32 devices in a mesh: col: 8 (over y, x, core), row: 4 (over z).
Axes of the slice: x: 2, y: 2, z: 4, core: 2. Of those that a mesh axis runs over, the one named last changes fastest.
Arguments:
- targets: float32 [4, 8, 1024, 128], P(None, 'col', 'row'), as said below
- src_panels: bfloat16 [512, 1024, 128], P('col', 'row')
- live_counts: int32 [8], P('col'), may hold values from 1 to 64, 256 in all
- dest_owner: int32 [512, 4], P('col'), may hold values from 0 to 7
- relative_map: int32 [512, 4, 8], P('col', None, 'row'), may hold values from 0 to 1, as said below
- diag_row: int32 [4, 8], replicated, may hold values from 0 to 3
- parent: int32 [3, 8], replicated, may hold values from 0 to 7
- chain_map: int32 [3, 8, 8], P(None, None, 'row'), may hold values from 0 to 1, as said below
Outputs:
- factors: float32 [4, 8, 1024, 128], P(None, 'col', 'row')
The draws below stay inside these ranges and needn't reach their ends.
Inputs may be any that keep to these rules, and one draw needn't show every extreme that they name: For each i, s and row group r, the 2 entries relative_map[i, s, r * 2 : (r + 1) * 2] are a permutation of 0 to 1; on r = diag_row[s, dest_owner[i, s]] it maps 0 to 0. For each s, k and row group r, the 2 entries chain_map[s, k, r * 2 : (r + 1) * 2] are a permutation of 0 to 1; on r = diag_row[s + 1, parent[s, k]] it maps 1 to 0. `live_counts`: the counts sum to 256 and the largest is 64. `targets`: every diagonal block after all updates is symmetric positive definite.
All inputs are finite; a program needn't handle non-finite values. No bound on the sum of `live_counts` on one device may be relied on, other than what follows from the above.
Results may differ from the reference program's by a relative error of at most 0.0003.
Values may be sent and summed in bfloat16 or wider, within the bound.
No kernel may reach another device: no remote copies, remote signals or barrier semaphores. Data moves between devices by JAX's collectives and lax.ppermute only.
A program may use at most 128 MiB of HBM per device.

```python
import math
import jax
import jax.numpy as jnp
import numpy as np
from jax import lax

B = 128
PB = 2
SRC = 64
STEPS = 4
N_COL = 8
N_ROW = 4


def permuted(key, leading, anchor, fixed):
    scores = jax.random.randint(key, leading + (PB,), 0, 1 << 20) * PB + jnp.arange(PB)
    ordered = jnp.argsort(scores, axis=-1, stable=True).astype(jnp.int32)
    partner = ordered[..., fixed:fixed + 1]
    swapped = jnp.where(ordered == 0, partner, ordered)
    swapped = jnp.where(jnp.arange(PB) == fixed, 0, swapped)
    groups = jnp.arange(N_ROW)[:, None]
    chosen = jnp.where(groups == anchor[..., None, None], swapped, ordered)
    return chosen.reshape(leading[:-1] + (N_ROW * PB,)).astype(jnp.int32)


def structure(key):
    folded = jax.random.fold_in(key, 4242)
    streams = jax.random.split(folded, 5)
    diag_row = jax.random.randint(streams[0], (STEPS, N_COL), 0, N_ROW).astype(jnp.int32)
    parent = jax.random.randint(streams[1], (STEPS - 1, N_COL), 0, N_COL).astype(jnp.int32)
    dest_owner = jax.random.randint(streams[2], (N_COL * SRC, STEPS), 0, N_COL).astype(jnp.int32)
    source_root = diag_row[jnp.arange(STEPS)[None, :], dest_owner]
    relative_map = permuted(streams[3], (N_COL * SRC, STEPS, N_ROW), source_root, 0)
    parent_root = diag_row[1:][jnp.arange(STEPS - 1)[:, None], parent]
    chain_map = permuted(streams[4], (STEPS - 1, N_COL, N_ROW), parent_root, 1)
    return (diag_row, parent, dest_owner, relative_map, chain_map)


def draw_diag_row(key, part):
    return structure(key)[0]


def draw_parent(key, part):
    return structure(key)[1]


def draw_dest_owner(key, part):
    return structure(key)[2]


def draw_relative_map(key, part):
    return structure(key)[3]


def draw_chain_map(key, part):
    return structure(key)[4]


def draw_src_panels(key, part):
    sigma = (SRC * B * 0.5) ** (-0.25)
    inner = jax.random.fold_in(key, 55)
    shape = (N_COL * SRC, N_ROW * PB * B, B)
    values = jax.random.truncated_normal(inner, -6.0, 6.0, shape, jnp.float32)
    return (values * sigma).astype(jnp.bfloat16)


def draw_targets(key, part):
    diag_row = structure(key)[0]
    streams = jax.random.split(jax.random.fold_in(key, 77), 3)
    level_base = math.sqrt(SRC * B * 0.5)
    off_scale = min(8.0, 0.75 * level_base / math.sqrt(B))
    shape = (STEPS, N_COL, N_ROW * PB, B, B)
    blocks = off_scale * jax.random.truncated_normal(streams[0], -6.0, 6.0, shape, jnp.float32)
    noise = jax.random.normal(streams[1], (STEPS, N_COL, B, B), jnp.float32)
    noise = (noise + jnp.swapaxes(noise, -1, -2)) * (0.15 * 6.5 * level_base / math.sqrt(2.0 * B))
    level = jax.random.uniform(streams[2], (STEPS, N_COL, 1, 1), jnp.float32, 6.0, 7.0) * level_base
    diagonal = noise + level * jnp.eye(B, dtype=jnp.float32)
    marked = jnp.arange(N_ROW * PB)[None, None, :] == (diag_row * PB)[:, :, None]
    combined = jnp.where(marked[..., None, None], diagonal[:, :, None], blocks)
    return combined.reshape(STEPS, N_COL, N_ROW * PB * B, B)


def length_profile(number_of, total, reach, skew):
    loads = [(1 << 20) // math.isqrt(rank ** skew) + 1 for rank in range(2, number_of + 1)]
    rest, holding = total - reach - (number_of - 1), [1] * (number_of - 1)
    while rest > 0:
        movable = [i for i in range(number_of - 1) if holding[i] < reach]
        pool, budget = sum([loads[i] for i in movable]), rest
        for i in movable:
            addition = min(reach - holding[i], max(1, budget * loads[i] // pool), rest)
            holding[i] = holding[i] + addition
            rest = rest - addition
    return np.array([reach] + holding)


def uneven(own_key, count, total, most, lean):
    if count == 2:
        one = jax.random.randint(own_key, (), max(1, total - most), min(most, total - 1) + 1)
        return jnp.stack([one, total - one])
    lengths = jnp.asarray(length_profile(count, total, most, lean), jnp.int32)
    pairs = (count - 1) // 2
    giver, taker = lengths[1:1 + 2 * pairs:2], lengths[2:2 + 2 * pairs:2]
    slack = jnp.minimum(giver - 1, most - taker)
    passed = jax.random.randint(jax.random.fold_in(own_key, 1), (pairs,), 0, 1 << 20) % (slack + 1)
    lengths = lengths.at[1:1 + 2 * pairs:2].set(giver - passed).at[2:2 + 2 * pairs:2].set(taker + passed)
    return lengths[jax.random.permutation(jax.random.fold_in(own_key, 2), count)]


def setup_inputs(seed: int = 0) -> dict:
    seeds = jax.random.split(jax.random.key(seed), 9)
    return {
        "targets": draw_targets(jax.random.fold_in(seeds[8], 71), 0),
        "src_panels": draw_src_panels(jax.random.fold_in(seeds[8], 71), 0),
        "live_counts": uneven(seeds[2], N_COL, N_COL * SRC // 2, SRC, 2).astype(jnp.int32),
        "dest_owner": draw_dest_owner(jax.random.fold_in(seeds[8], 71), 0),
        "relative_map": draw_relative_map(jax.random.fold_in(seeds[8], 71), 0),
        "diag_row": draw_diag_row(jax.random.fold_in(seeds[8], 71), 0),
        "parent": draw_parent(jax.random.fold_in(seeds[8], 71), 0),
        "chain_map": draw_chain_map(jax.random.fold_in(seeds[8], 71), 0),
    }


def lower_solve(lower_block, blocks):
    return lax.linalg.triangular_solve(jnp.broadcast_to(lower_block[:, None], blocks.shape), blocks, left_side=False, lower=True, transpose_a=True)

def reference(targets, src_panels, live_counts, dest_owner, relative_map, diag_row, parent, chain_map):
    total_blocks = N_ROW * PB
    owners = jnp.arange(N_COL)
    panels = src_panels.reshape(N_COL, SRC, total_blocks, B, B)
    alive_mask = (jnp.arange(SRC)[None, :] < live_counts[:, None]).astype(jnp.float32)
    group_of = (jnp.arange(total_blocks) // PB).astype(jnp.int32)
    source_root = diag_row[jnp.arange(STEPS)[None, :], dest_owner].reshape(N_COL, SRC, STEPS)
    dest_grid = dest_owner.reshape(N_COL, SRC, STEPS)
    map_grid = relative_map.reshape(N_COL, SRC, STEPS, total_blocks)
    results = []
    for s in range(STEPS):

        def add_owner(running, inputs):
            panel_set, root_rows, targets_of, local_map, alive_row = inputs
            columns = panel_set[jnp.arange(SRC), root_rows * PB]
            products = jnp.einsum('ijab,icb->ijac', panel_set.astype(jnp.float32), columns.astype(jnp.float32))
            products = products * alive_row[:, None, None, None]
            slot_ids = targets_of[:, None] * total_blocks + group_of[None, :] * PB + local_map
            summed = jax.ops.segment_sum(products.reshape(SRC * total_blocks, B, B), slot_ids.reshape(-1), num_segments=N_COL * total_blocks)
            return (running + summed, None)
        update = lax.scan(add_owner, jnp.zeros((N_COL * total_blocks, B, B), jnp.float32), (panels, source_root[:, :, s], dest_grid[:, :, s], map_grid[:, :, s], alive_mask))[0]
        if s > 0:
            child_rows = results[-1].astype(jnp.bfloat16).reshape(N_COL, total_blocks, B, B)
            parent_root = diag_row[s, parent[s - 1]]
            column = child_rows[owners, parent_root * PB + 1]
            products = jnp.einsum('kjab,kcb->kjac', child_rows.astype(jnp.float32), column.astype(jnp.float32))
            kept_mask = jnp.arange(total_blocks)[None, :] != (diag_row[s - 1] * PB)[:, None]
            products = products * kept_mask[:, :, None, None].astype(jnp.float32)
            slot_ids = parent[s - 1][:, None] * total_blocks + group_of[None, :] * PB + chain_map[s - 1]
            update = update + jax.ops.segment_sum(products.reshape(N_COL * total_blocks, B, B), slot_ids.reshape(-1), num_segments=N_COL * total_blocks)
        updated = targets[s].reshape(N_COL, total_blocks, B, B) - update.reshape(N_COL, total_blocks, B, B)
        root_block = diag_row[s] * PB
        lower_block = jnp.linalg.cholesky(updated[owners, root_block])
        solved = lower_solve(lower_block, updated)
        is_diag = (jnp.arange(total_blocks)[None, :] == root_block[:, None])[:, :, None, None]
        factor = jnp.where(is_diag, lower_block[:, None], solved)
        results.append(factor.reshape(N_COL, total_blocks * B, B))
    return jnp.stack(results)
```

```python
import functools

import jax
import jax.numpy as jnp
from jax import lax
from jax.experimental import pallas as pl
from jax.experimental.pallas import tpu as pltpu
from jax.sharding import PartitionSpec as P

F32 = jnp.float32
BF16 = jnp.bfloat16
HIGHEST = lax.Precision.HIGHEST
CHUNK = 8
PANEL = 32
VMEM_LIMIT = 48 * 1024 * 1024


def vmem():
    return pl.BlockSpec(memory_space=pltpu.VMEM)


def smem():
    return pl.BlockSpec(memory_space=pltpu.SMEM)


def params():
    return pltpu.CompilerParams(vmem_limit_bytes=VMEM_LIMIT)


def cost(flops, size):
    return pl.CostEstimate(flops=flops, bytes_accessed=size, transcendentals=0)


def times_transposed(a, b, precision=None):
    return lax.dot_general(
        a, b, (((1,), (1,)), ((), ())), precision=precision, preferred_element_type=F32
    )


def transposed_times(a, b):
    return lax.dot_general(a, b, (((0,), (0,)), ((), ())), preferred_element_type=F32)


def slot_column(slot, chips, own):
    return own ^ (2 * (slot % chips) + slot // chips)


def swap(x, axis, size, mask):
    return lax.ppermute(x, axis, [(i, i ^ mask) for i in range(size)])


def gather_columns(x, col_count):
    chips = col_count // 2
    same = [x] + [swap(x, "col", col_count, 2 * m) for m in range(1, chips)]
    return same + [swap(y, "col", col_count, 1) for y in same]


def scatter_sum(other_half, own_half, col_count):
    chips = col_count // 2
    summed = own_half + swap(other_half, "col", col_count, 1)
    parts = [summed[0]]
    for m in range(1, chips):
        parts.append(swap(summed[m], "col", col_count, 2 * m))
    return parts


def spread(x, roots, row_index, row_count):
    roots = roots.reshape(roots.shape + (1,) * (x.ndim - 1))
    mine = roots == row_index
    up, down = x, x
    for _ in range(row_count - 1):
        up = jnp.where(mine, x, lax.ppermute(up, "row", [(i, i + 1) for i in range(row_count - 1)]))
        down = jnp.where(
            mine, x, lax.ppermute(down, "row", [(i + 1, i) for i in range(row_count - 1)])
        )
    return jnp.where(roots <= row_index, up, down)


def tables_kernel(col_count, place, diag, parent, chain, roots, picks, ahead, keep, into):
    sections = diag.shape[0]
    local_blocks = chain.shape[3]
    chips = col_count // 2
    own = place[0]
    row = place[1]

    def path(s, column):
        columns = [column]
        for t in range(s, sections - 1):
            columns.append(parent[t, columns[-1]])
        return columns

    def block_of(s, columns, j):
        if j == 0:
            return jnp.int32(0)
        if j == 1:
            return jnp.int32(1)
        wanted = block_of(s + 1, columns[1:], j - 1)
        group = diag[s + j, columns[j]]
        found = jnp.int32(0)
        for q in range(1, local_blocks):
            found = jnp.where(chain[group, s, columns[0], q] == wanted, q, found)
        return found

    for s in range(sections):
        columns = path(s, own)
        for j in range(sections):
            if j < sections - s:
                roots[s, j] = diag[s + j, columns[j]]
                picks[s, j] = block_of(s, columns, j)
            else:
                roots[s, j] = 0
                picks[s, j] = 0
    for s in range(1, sections):
        for slot in range(col_count):
            child = slot_column(slot, chips, own)
            hit = parent[s - 1, child] == own
            columns = path(s - 1, child)
            for j in range(sections):
                if j < sections - s:
                    block = block_of(s - 1, columns, j + 1)
                    group = diag[s + j, columns[j + 1]]
                    left_out = (block == 0) & (group == diag[s - 1, child])
                    ahead[s, slot, j] = jnp.where(hit & jnp.logical_not(left_out), 1, 0)
                else:
                    ahead[s, slot, j] = 0
            for q in range(local_blocks):
                left_out = (diag[s - 1, child] == row) & (q == 0)
                keep[s, slot, q] = jnp.where(hit & jnp.logical_not(left_out), 1, 0)
                into[s, slot, q] = chain[row, s - 1, child, q]


def source_kernel(local_blocks, col_count, step, table, live, panels, heads, other, own, total):
    g = pl.program_id(0)
    width = panels.shape[2]
    chips = col_count // 2

    @pl.when(g == 0)
    def _():
        total[...] = jnp.zeros_like(total)

    @pl.when(g * CHUNK < live[0])
    def _():
        for t in range(CHUNK):
            i = g * CHUNK + t
            slot = table[step, 0, i]
            head = heads[table[step, 1, i], t]
            product = times_transposed(panels[t], head)
            for q in range(local_blocks):
                p = table[step, 2 + q, i]
                total[slot, p] += product[q * width : (q + 1) * width]
            total[slot, local_blocks] += times_transposed(head, head)

    @pl.when(g == pl.num_programs(0) - 1)
    def _():
        own[...] = total[:chips]
        other[...] = total[chips : 2 * chips]


def source_sums(step, table, live, panels, heads, col_count):
    count, rows, width = panels.shape
    local_blocks = rows // width
    row_count = heads.shape[0]
    chips = col_count // 2
    half = (chips, local_blocks + 1, width, width)

    def chunk(g, table, live):
        return jnp.minimum(g, (live[0] - 1) // CHUNK)

    out = jax.ShapeDtypeStruct(half, F32)
    return pl.pallas_call(
        functools.partial(source_kernel, local_blocks, col_count, step),
        grid_spec=pltpu.PrefetchScalarGridSpec(
            num_scalar_prefetch=2,
            grid=(count // CHUNK,),
            in_specs=[
                pl.BlockSpec((CHUNK, rows, width), lambda g, a, b: (chunk(g, a, b), 0, 0)),
                pl.BlockSpec(
                    (row_count, CHUNK, width, width), lambda g, a, b: (0, chunk(g, a, b), 0, 0)
                ),
            ],
            out_specs=[pl.BlockSpec(half, lambda g, a, b: (0, 0, 0, 0))] * 2,
            scratch_shapes=[pltpu.VMEM((2 * chips + 1,) + half[1:], F32)],
        ),
        out_shape=[out, out],
        compiler_params=params(),
        cost_estimate=cost(count * (rows + width) * width * width * 2, count * rows * width * 4),
        name="source_sums",
    )(table, live, panels, heads)


def split(x):
    high = x.astype(BF16)
    rest = x - high.astype(F32)
    middle = rest.astype(BF16)
    low = (rest - middle.astype(F32)).astype(BF16)
    return high, middle, low


def factor_kernel(step, col_count, flags, start, *refs):
    children, (upper, inverse, work) = refs[:-3], refs[-3:]
    width = start.shape[0]
    work[:, :width] = start[...]
    for slot, child in enumerate(children):

        @pl.when(flags[step, slot, 0] > 0)
        def _(child=child):
            work[:, :width] -= times_transposed(child[0], child[0])

    rows = lax.broadcasted_iota(jnp.int32, (width, width), 0)
    columns = lax.broadcasted_iota(jnp.int32, (width, width), 1)
    work[:, width:] = (rows == columns).astype(F32)
    sub = lax.broadcasted_iota(jnp.int32, (PANEL, 1), 0)
    for first in range(0, width, PANEL):
        last = first + PANEL
        slab = work[first:last, :]
        spans = [
            jnp.broadcast_to(slab[:, first + k : first + k + 1], (PANEL, width))
            for k in range(PANEL)
        ]
        scale = jnp.zeros((PANEL, 1), F32)
        for j in range(PANEL):
            pivot = spans[j][j : j + 1, :]
            ratio = jnp.where(sub > j, spans[j] * (1.0 / pivot), 0.0)
            for k in range(j + 1, PANEL):
                spans[k] = spans[k] - ratio * spans[k][j : j + 1, :]
            slab = slab - jnp.concatenate([ratio, ratio], axis=1) * slab[j : j + 1, :]
            scale = jnp.where(sub == j, lax.rsqrt(pivot[:, 0:1]), scale)
        slab = slab * scale
        work[first:last, :] = slab
        if last < width:
            high, middle, low = split(slab)
            left = jnp.concatenate([high, high, middle, middle, high, low], axis=0)
            right = jnp.concatenate([high, middle, high, middle, low, high], axis=0)
            work[last:, :] = work[last:, :] - transposed_times(left[:, last:width], right)
    upper[...] = jnp.where(rows <= columns, work[:, :width], 0.0)
    inverse[...] = work[:, width:]


def factor(step, flags, start, children, col_count):
    width = start.shape[0]
    out = jax.ShapeDtypeStruct((width, width), F32)
    return pl.pallas_call(
        functools.partial(factor_kernel, step, col_count),
        in_specs=[smem(), vmem()] + [vmem()] * len(children),
        out_specs=[vmem(), vmem()],
        out_shape=[out, out],
        scratch_shapes=[pltpu.VMEM((width, 2 * width), F32)],
        compiler_params=params(),
        cost_estimate=cost(width * width * width * 200, 16 * width * width),
        name="factor",
    )(flags, start, *children)


def ahead_kernel(step, flags, start, inverse, *refs):
    children, (out, work) = refs[:-2], refs[-2:]
    work[...] = start[...]
    for j in range(start.shape[0]):
        for slot, child in enumerate(children):

            @pl.when(flags[step, slot, j + 1] > 0)
            def _(child=child, j=j):
                work[j] -= times_transposed(child[j + 1], child[0])

        out[j] = times_transposed(work[j], inverse[...], HIGHEST).astype(BF16)


def ahead_blocks(step, flags, start, inverse, children):
    return pl.pallas_call(
        functools.partial(ahead_kernel, step),
        in_specs=[smem(), vmem(), vmem()] + [vmem()] * len(children),
        out_specs=vmem(),
        out_shape=jax.ShapeDtypeStruct(start.shape, BF16),
        scratch_shapes=[pltpu.VMEM(start.shape, F32)],
        compiler_params=params(),
        cost_estimate=cost(start.size * 2000, start.size * 8),
        name="ahead_blocks",
    )(flags, start, inverse, *children)


def panel_kernel(step, child_count, place, roots, keep, into, start, inverse, upper, *refs):
    columns, panels = refs[:child_count], refs[child_count : 2 * child_count]
    out, rounded, work = refs[2 * child_count :]
    blocks, width = start.shape[0], start.shape[1]
    work[...] = start[...]
    for slot in range(child_count):
        for q in range(blocks):

            @pl.when(keep[step, slot, q] > 0)
            def _(slot=slot, q=q):
                work[into[step, slot, q]] -= times_transposed(panels[slot][q], columns[slot][0])

    for q in range(blocks):
        solved = times_transposed(work[q], inverse[...], HIGHEST)
        out[q * width : (q + 1) * width, :] = solved
        rounded[q] = solved.astype(BF16)

    @pl.when(place[1] == roots[step, 0])
    def _():
        out[:width, :] = upper[...].T


def panel_rows(step, place, roots, keep, into, start, inverse, upper, columns, panels):
    blocks, width, _ = start.shape
    return pl.pallas_call(
        functools.partial(panel_kernel, step, len(columns)),
        in_specs=[smem()] * 4 + [vmem()] * (3 + len(columns) + len(panels)),
        out_specs=[vmem(), vmem()],
        out_shape=[
            jax.ShapeDtypeStruct((blocks * width, width), F32),
            jax.ShapeDtypeStruct(start.shape, BF16),
        ],
        scratch_shapes=[pltpu.VMEM(start.shape, F32)],
        compiler_params=params(),
        cost_estimate=cost(start.size * 2000, start.size * 16),
        name="panel_rows",
    )(place, roots, keep, into, start, inverse, upper, *columns, *panels)


def local(targets, src_panels, live_counts, dest_owner, relative_map, diag_row, parent, chain_map):
    col_count = lax.axis_size("col")
    row_count = lax.axis_size("row")
    own = lax.axis_index("col")
    row_index = lax.axis_index("row")
    chips = col_count // 2
    src_count, _, width = src_panels.shape
    local_blocks = src_panels.shape[1] // width
    sections = targets.shape[0]
    targets = targets.reshape(sections, local_blocks, width, width)

    heads = lax.all_gather(src_panels[:, :width][None], "row", axis=0, tiled=True)

    place = jnp.stack([own, row_index]).astype(jnp.int32)
    chain = lax.all_gather(chain_map[None], "row", axis=0, tiled=True)
    tab = functools.partial(jax.ShapeDtypeStruct, dtype=jnp.int32)
    roots, picks, ahead, keep, into = pl.pallas_call(
        functools.partial(tables_kernel, col_count),
        in_specs=[smem()] * 4,
        out_specs=[smem()] * 5,
        out_shape=[
            tab((sections, sections)),
            tab((sections, sections)),
            tab((sections, col_count, sections)),
            tab((sections, col_count, local_blocks)),
            tab((sections, col_count, local_blocks)),
        ],
        name="tables",
    )(place, diag_row, parent, chain)

    alive = jnp.arange(src_count)[:, None] < live_counts[0]
    offset = jnp.bitwise_xor(dest_owner, own)
    slots = jnp.where(alive, (offset % 2) * chips + offset // 2, 2 * chips)
    source_root = diag_row[jnp.arange(sections)[None, :], dest_owner]
    table = jnp.concatenate(
        [slots.T[:, None], source_root.T[:, None], relative_map.transpose(1, 2, 0)], axis=1
    ).astype(jnp.int32)

    diagonal_targets = spread(targets[:, 0], roots[:, 0], row_index, row_count)

    starts = []
    for s in range(sections):
        other, mine = source_sums(s, table, live_counts, src_panels, heads, col_count)
        parts = scatter_sum(other, mine, col_count)
        total = functools.reduce(jnp.add, parts)
        panel = targets[s] - total[:local_blocks]
        diagonal = diagonal_targets[s] - total[local_blocks]
        later = None
        if s + 1 < sections:
            picked = panel[picks[s, 1 : sections - s]]
            later = spread(picked, roots[s, 1 : sections - s], row_index, row_count)
        starts.append((panel, diagonal, later))

    results = []
    columns, panels = [], []
    for s in range(sections):
        panel, diagonal, later = starts[s]
        upper, inverse = factor(s, ahead, diagonal, columns, col_count)
        rows, rounded = panel_rows(
            s, place, roots, keep, into, panel, inverse, upper, columns, panels
        )
        results.append(rows)
        if s + 1 < sections:
            needed = ahead_blocks(s, ahead, later, inverse, columns)
            columns = gather_columns(needed, col_count)
            panels = gather_columns(rounded, col_count)
    return jnp.stack(results)[:, None]


def solution(mesh):
    return jax.shard_map(
        local,
        mesh=mesh,
        in_specs=(
            P(None, "col", "row", None),
            P("col", "row", None),
            P("col"),
            P("col", None),
            P("col", None, "row"),
            P(),
            P(),
            P(None, None, "row"),
        ),
        out_specs=P(None, "col", "row", None),
        check_vma=False,
    )
```

```python
import functools

import jax
import jax.numpy as jnp
from jax import lax
from jax.experimental import pallas as pl
from jax.experimental.pallas import tpu as pltpu
from jax.sharding import PartitionSpec as P

F32 = jnp.float32
BF16 = jnp.bfloat16
HIGHEST = lax.Precision.HIGHEST
CHUNK = 8
PANEL = 32
MIB = 1024 * 1024


def vmem():
    return pl.BlockSpec(memory_space=pltpu.VMEM)


def smem():
    return pl.BlockSpec(memory_space=pltpu.SMEM)


def params(mib):
    return pltpu.CompilerParams(vmem_limit_bytes=mib * MIB)


def cost(flops, size):
    return pl.CostEstimate(flops=flops, bytes_accessed=size, transcendentals=0)


def times_transposed(a, b, precision=None):
    return lax.dot_general(
        a, b, (((1,), (1,)), ((), ())), precision=precision, preferred_element_type=F32
    )


def transposed_times(a, b):
    return lax.dot_general(a, b, (((0,), (0,)), ((), ())), preferred_element_type=F32)


def slot_column(slot, chips, own):
    return own ^ (2 * (slot % chips) + slot // chips)


def swap(x, axis, size, mask):
    return lax.ppermute(x, axis, [(i, i ^ mask) for i in range(size)])


def gather_columns(x, col_count):
    chips = col_count // 2
    same = [x] + [swap(x, "col", col_count, 2 * m) for m in range(1, chips)]
    return same + [swap(y, "col", col_count, 1) for y in same]


def scatter_sum(other_half, own_half, col_count):
    chips = col_count // 2
    halves = own_half + swap(other_half, "col", col_count, 1)
    whole = halves[0]
    for m in range(1, chips):
        whole = whole + swap(halves[m], "col", col_count, 2 * m)
    return halves, whole


def tables_kernel(col_count, place, diag, parent, chain, roots, picks, ahead, keep, into):
    sections = diag.shape[0]
    local_blocks = chain.shape[3]
    chips = col_count // 2
    own = place[0]
    row = place[1]

    def path(s, column):
        columns = [column]
        for t in range(s, sections - 1):
            columns.append(parent[t, columns[-1]])
        return columns

    def block_of(s, columns, j):
        if j == 0:
            return jnp.int32(0)
        if j == 1:
            return jnp.int32(1)
        wanted = block_of(s + 1, columns[1:], j - 1)
        group = diag[s + j, columns[j]]
        found = jnp.int32(0)
        for q in range(1, local_blocks):
            found = jnp.where(chain[group, s, columns[0], q] == wanted, q, found)
        return found

    for s in range(sections):
        columns = path(s, own)
        for j in range(sections):
            if j < sections - s:
                roots[s, j] = diag[s + j, columns[j]]
                picks[s, j] = block_of(s, columns, j)
            else:
                roots[s, j] = 0
                picks[s, j] = 0
    for s in range(1, sections):
        for slot in range(col_count):
            child = slot_column(slot, chips, own)
            hit = parent[s - 1, child] == own
            columns = path(s - 1, child)
            for j in range(sections):
                if j < sections - s:
                    block = block_of(s - 1, columns, j + 1)
                    group = diag[s + j, columns[j + 1]]
                    left_out = (block == 0) & (group == diag[s - 1, child])
                    ahead[s, slot, j] = jnp.where(hit & jnp.logical_not(left_out), 1, 0)
                else:
                    ahead[s, slot, j] = 0
            for q in range(local_blocks):
                left_out = (diag[s - 1, child] == row) & (q == 0)
                keep[s, slot, q] = jnp.where(hit & jnp.logical_not(left_out), 1, 0)
                into[s, slot, q] = chain[row, s - 1, child, q]


def pick_kernel(index, source, out):
    for i in range(out.shape[0]):
        out[i] = source[index[i]]


def pick(source, index, block, rows):
    count, width = index.shape[0], source.shape[2]
    return pl.pallas_call(
        pick_kernel,
        grid_spec=pltpu.PrefetchScalarGridSpec(
            num_scalar_prefetch=1,
            grid=(1,),
            in_specs=[pl.BlockSpec((source.shape[0], rows, width), lambda g, a: (0, block, 0))],
            out_specs=pl.BlockSpec((count, rows, width), lambda g, a: (0, 0, 0)),
        ),
        out_shape=jax.ShapeDtypeStruct((count, rows, width), source.dtype),
        compiler_params=params(12),
        cost_estimate=cost(0, 4 * count * rows * width),
        name="pick",
    )(index, source)


def diagonal_kernel(table, heads, other, own, total):
    g = pl.program_id(0)
    chips = own.shape[0]
    sections = table.shape[0]

    @pl.when(g == 0)
    def _():
        total[...] = jnp.zeros_like(total)

    for t in range(heads.shape[0]):
        product = times_transposed(heads[t], heads[t])
        for s in range(sections):
            total[table[s, 0, g * heads.shape[0] + t], s] += product

    @pl.when(g == pl.num_programs(0) - 1)
    def _():
        own[...] = total[:chips]
        other[...] = total[chips : 2 * chips]


def diagonal_sums(table, heads, chips):
    count, width, _ = heads.shape
    sections = table.shape[0]
    chunk = min(CHUNK, count)
    half = (chips, sections, width, width)
    out = jax.ShapeDtypeStruct(half, F32)
    return pl.pallas_call(
        diagonal_kernel,
        grid_spec=pltpu.PrefetchScalarGridSpec(
            num_scalar_prefetch=1,
            grid=(count // chunk,),
            in_specs=[pl.BlockSpec((chunk, width, width), lambda g, a: (g, 0, 0))],
            out_specs=[pl.BlockSpec(half, lambda g, a: (0, 0, 0, 0))] * 2,
            scratch_shapes=[pltpu.VMEM((2 * chips + 1,) + half[1:], F32)],
        ),
        out_shape=[out, out],
        compiler_params=params(6 * chips * sections * width * width * 4 // MIB + 8),
        cost_estimate=cost(count * width * width * width * 4, count * width * width * 4),
        name="diagonal_sums",
    )(table, heads)


def source_kernel(table, first, second, heads, after, other, own, total):
    del after
    g = pl.program_id(0)
    chunk, width, _ = first.shape
    chips = own.shape[0]
    blocks = second.shape[1] + 1
    sections = table.shape[0]

    @pl.when(g == 0)
    def _():
        total[...] = jnp.zeros_like(total)

    for t in range(chunk):
        i = g * chunk + t
        panel = jnp.concatenate([first[t]] + [second[t, q] for q in range(blocks - 1)], axis=0)
        for begin in range(0, sections, 2):
            steps = range(begin, min(begin + 2, sections))
            stacked = jnp.concatenate([heads[table[s, 1, i], t] for s in steps], axis=0)
            product = times_transposed(panel, stacked)
            for k, s in enumerate(steps):
                slot = table[s, 0, i]
                for q in range(blocks):
                    total[slot, s * blocks + table[s, 2 + q, i]] += product[
                        q * width : (q + 1) * width, k * width : (k + 1) * width
                    ]

    @pl.when(g == pl.num_programs(0) - 1)
    def _():
        other[...] = total[chips : 2 * chips]
        own[...] = total[:chips]


def source_sums(table, first, second, heads, after, chips):
    count, width, _ = first.shape
    blocks = 1 + second.shape[1]
    sections = table.shape[0]
    chunk = min(CHUNK, count)
    half = (chips, sections * blocks, width, width)
    out = jax.ShapeDtypeStruct(half, F32)
    size = 4 * chips * sections * blocks * width * width
    return pl.pallas_call(
        source_kernel,
        grid_spec=pltpu.PrefetchScalarGridSpec(
            num_scalar_prefetch=1,
            grid=(count // chunk,),
            in_specs=[
                pl.BlockSpec((chunk, width, width), lambda g, a: (g, 0, 0)),
                pl.BlockSpec((chunk, blocks - 1, width, width), lambda g, a: (g, 0, 0, 0)),
                pl.BlockSpec((heads.shape[0], chunk, width, width), lambda g, a: (0, g, 0, 0)),
                pl.BlockSpec(memory_space=pl.ANY),
            ],
            out_specs=[pl.BlockSpec(half, lambda g, a: (0, 0, 0, 0))] * 2,
            scratch_shapes=[pltpu.VMEM((2 * chips,) + half[1:], F32)],
        ),
        out_shape=[out, out],
        compiler_params=params(6 * size // MIB + 12),
        cost_estimate=cost(
            count * blocks * width * width * width * 2 * sections, count * width * width * 12
        ),
        name="source_sums",
    )(table, first, second, heads, after)


def split(x):
    high = x.astype(BF16)
    rest = x - high.astype(F32)
    middle = rest.astype(BF16)
    low = (rest - middle.astype(F32)).astype(BF16)
    return high, middle, low


def factor_kernel(step, col_count, flags, start, *refs):
    children, (upper, inverse, work) = refs[:-3], refs[-3:]
    width = start.shape[0]
    work[:, :width] = start[...]
    for slot, child in enumerate(children):

        @pl.when(flags[step, slot, 0] > 0)
        def _(child=child):
            work[:, :width] -= times_transposed(child[0], child[0])

    rows = lax.broadcasted_iota(jnp.int32, (width, width), 0)
    columns = lax.broadcasted_iota(jnp.int32, (width, width), 1)
    work[:, width:] = (rows == columns).astype(F32)
    sub = lax.broadcasted_iota(jnp.int32, (PANEL, 1), 0)
    for first in range(0, width, PANEL):
        last = first + PANEL
        slab = work[first:last, :]
        spans = [
            jnp.broadcast_to(slab[:, first + k : first + k + 1], (PANEL, width))
            for k in range(PANEL)
        ]
        scale = jnp.zeros((PANEL, 1), F32)
        for j in range(PANEL):
            pivot = spans[j][j : j + 1, :]
            ratio = jnp.where(sub > j, spans[j] * (1.0 / pivot), 0.0)
            for k in range(j + 1, PANEL):
                spans[k] = spans[k] - ratio * spans[k][j : j + 1, :]
            slab = slab - jnp.concatenate([ratio, ratio], axis=1) * slab[j : j + 1, :]
            scale = jnp.where(sub == j, lax.rsqrt(pivot[:, 0:1]), scale)
        slab = slab * scale
        work[first:last, :] = slab
        if last < width:
            high, middle, low = split(slab)
            left = jnp.concatenate([high, high, middle, middle, high, low], axis=0)
            right = jnp.concatenate([high, middle, high, middle, low, high], axis=0)
            work[last:, :] = work[last:, :] - transposed_times(left[:, last:width], right)
    upper[...] = jnp.where(rows <= columns, work[:, :width], 0.0)
    inverse[...] = work[:, width:]


def factor(step, flags, start, children, col_count):
    width = start.shape[0]
    out = jax.ShapeDtypeStruct((width, width), F32)
    return pl.pallas_call(
        functools.partial(factor_kernel, step, col_count),
        in_specs=[smem(), vmem()] + [vmem()] * len(children),
        out_specs=[vmem(), vmem()],
        out_shape=[out, out],
        scratch_shapes=[pltpu.VMEM((width, 2 * width), F32)],
        compiler_params=params(8),
        cost_estimate=cost(width * width * width * 200, 16 * width * width),
        name="factor",
    )(flags, start, *children)


def blocks_kernel(
    step, ahead, send, place, roots, flags, keep, into, after, start, inverse, upper, *refs
):
    del after
    work, refs = refs[-1], refs[:-1]
    rounded, refs = (refs[-1], refs[:-1]) if send else (None, refs)
    out, refs = refs[-1], refs[:-1]
    later, children = (refs[0], refs[1:]) if ahead else (None, refs)
    blocks, width = start.shape[0], start.shape[1]
    for j in range(ahead):
        work[j] = later[j]
    work[ahead:] = start[...]
    for slot, child in enumerate(children):
        skipped = child.shape[0] - blocks
        for j in range(ahead):

            @pl.when(flags[step, slot, j + 1] > 0)
            def _(slot=slot, child=child, j=j):
                work[j] -= times_transposed(child[j + 1], child[0])

        for q in range(blocks):

            @pl.when(keep[step, slot, q] > 0)
            def _(slot=slot, child=child, q=q):
                work[ahead + into[step, slot, q]] -= times_transposed(
                    child[skipped + q], child[0]
                )

    solved = times_transposed(
        work[...].reshape((ahead + blocks) * width, width), inverse[...], HIGHEST
    )
    out[...] = solved[ahead * width :]
    if send:
        rounded[...] = solved.astype(BF16).reshape(ahead + blocks, width, width)

    @pl.when(place[1] == roots[step, 0])
    def _():
        out[:width, :] = upper[...].T


def panel_blocks(step, tables, after, start, later, send, inverse, upper, children):
    blocks, width, _ = start.shape
    ahead = 0 if later is None else later.shape[0]
    arrays = [start, inverse, upper] + ([later] if ahead else []) + list(children)
    out = [jax.ShapeDtypeStruct((blocks * width, width), F32)]
    if send:
        out.append(jax.ShapeDtypeStruct((ahead + blocks, width, width), BF16))
    return pl.pallas_call(
        functools.partial(blocks_kernel, step, ahead, send),
        in_specs=[smem()] * len(tables)
        + [pl.BlockSpec(memory_space=pl.ANY)]
        + [vmem()] * len(arrays),
        out_specs=[vmem()] * len(out),
        out_shape=out,
        scratch_shapes=[pltpu.VMEM((blocks + ahead, width, width), F32)],
        compiler_params=params(12),
        cost_estimate=cost(start.size * 2000, start.size * 16),
        name="panel_blocks",
    )(*tables, after, *arrays)


def local(targets, src_panels, live_counts, dest_owner, relative_map, diag_row, parent, chain_map):
    col_count = lax.axis_size("col")
    row_count = lax.axis_size("row")
    own = lax.axis_index("col")
    row_index = lax.axis_index("row")
    chips = col_count // 2
    src_count, _, width = src_panels.shape
    local_blocks = src_panels.shape[1] // width
    sections = targets.shape[0]
    targets = targets.reshape(sections, local_blocks, width, width)

    place = jnp.stack([own, row_index]).astype(jnp.int32)

    dealt = src_count // 2
    share = src_count // col_count
    facts = jnp.concatenate(
        [
            dest_owner.T,
            relative_map.transpose(1, 2, 0).reshape(sections * local_blocks, src_count),
            jnp.broadcast_to(live_counts, (1, src_count)),
        ],
        axis=0,
    ).astype(jnp.int32)
    facts = lax.all_gather(facts, "col", axis=0)
    counts = facts[:, -1, 0]
    columns_of = jnp.arange(col_count)
    offsets = jnp.sum(jnp.where(columns_of[None, :] < columns_of[:, None], counts[None, :], 0), axis=1)
    own_offset = jnp.sum(jnp.where(columns_of == own, offsets, 0))
    sent = (
        jnp.mod(columns_of - own_offset, col_count)[:, None]
        + col_count * jnp.arange(share)[None, :]
    ).reshape(-1)
    number = jnp.arange(dealt) * col_count + own
    source_column = jnp.sum(
        (offsets[None, :] <= number[:, None]).astype(jnp.int32), axis=1
    ) - 1
    index = number - jnp.sum(
        jnp.where(columns_of[None, :] == source_column[:, None], offsets[None, :], 0), axis=1
    )
    kept = source_column * share + index // col_count

    def deal(block):
        mixed = lax.all_to_all(pick(src_panels, sent, block, width), "col", 0, 0, tiled=True)
        return pick(mixed, kept, 0, width)

    first = deal(0)
    heads = lax.all_gather(first, "row", axis=0)
    second = jnp.stack([deal(q) for q in range(1, local_blocks)], axis=1)

    chain = lax.all_gather(chain_map[None], "row", axis=0, tiled=True)
    tab = functools.partial(jax.ShapeDtypeStruct, dtype=jnp.int32)
    roots, picks, ahead, keep, into = pl.pallas_call(
        functools.partial(tables_kernel, col_count),
        in_specs=[smem()] * 4,
        out_specs=[smem()] * 5,
        out_shape=[
            tab((sections, sections)),
            tab((sections, sections)),
            tab((sections, col_count, sections)),
            tab((sections, col_count, local_blocks)),
            tab((sections, col_count, local_blocks)),
        ],
        name="tables",
    )(place, diag_row, parent, chain)

    facts = facts.transpose(0, 2, 1).reshape(col_count * src_count, -1)
    facts = facts[source_column * src_count + index]
    dest = facts[:, :sections].T
    target_blocks = facts[:, sections:-1].T.reshape(sections, local_blocks, dealt)
    offset = jnp.bitwise_xor(dest, own)
    slots = (offset % 2) * chips + offset // 2
    source_root = jnp.sum(
        jnp.where(dest[:, :, None] == columns_of, diag_row[:, None, :], 0), axis=-1
    )
    table = jnp.concatenate([slots[:, None], source_root[:, None], target_blocks], axis=1)
    held = jnp.where(source_root == row_index, slots, 2 * chips)[:, None]

    other, mine = diagonal_sums(held, first, chips)
    _, total = scatter_sum(other, mine, col_count)

    def known(items):
        return jnp.stack([jnp.where(root == row_index, x, 0.0) for root, x in items])

    def share(x):
        return jnp.sum(lax.all_gather(x, "row", axis=0), axis=0)

    last = sections - 1
    soon = min(2, sections)
    items = [(roots[s, 0], targets[s, 0] - total[s]) for s in range(sections)]
    diagonals = share(known(items[:soon]))
    diagonals = [diagonals[s] for s in range(soon)]
    factored = factor(0, ahead, diagonals[0], [], col_count)

    sums = source_sums(table, first, second, heads, factored[0], chips)
    _, whole = scatter_sum(*sums, col_count)
    starts = targets - whole.reshape(targets.shape)

    later = [None] * sections
    pairs = [(s, j) for s in range(1, last) for j in range(1, sections - s)]
    group = known([(roots[s, j], starts[s][picks[s, j]]) for s, j in pairs] + items[soon:])
    whole = share(group)
    for s in range(1, last):
        at = pairs.index((s, 1))
        later[s] = whole[at : at + last - s]
    diagonals += [whole[len(pairs) + n] for n in range(sections - soon)]

    results, children = [], []
    tables = (place, roots, ahead, keep, into)
    for s in range(sections):
        upper, inverse = factored
        if s > 0:
            upper, inverse = factor(s, ahead, diagonals[s], children, col_count)
        made = panel_blocks(
            s, tables, group if s == 0 else place, starts[s], later[s], s < last, inverse, upper, children
        )
        results.append(made[0])
        if s < last:
            message = made[1]
            if s == 0:
                whole = lax.all_gather(message, "row", axis=0)
                needed = [whole[roots[0, j], picks[0, j]] for j in range(1, sections)]
                message = jnp.concatenate([jnp.stack(needed), message], axis=0)
            children = gather_columns(message, col_count)
    return jnp.stack(results)[:, None]


def solution(mesh):
    return jax.shard_map(
        local,
        mesh=mesh,
        in_specs=(
            P(None, "col", "row", None),
            P("col", "row", None),
            P("col"),
            P("col", None),
            P("col", None, "row"),
            P(),
            P(),
            P(None, None, "row"),
        ),
        out_specs=P(None, "col", "row", None),
        check_vma=False,
    )
```

```python
import functools

import jax
import jax.numpy as jnp
from jax import lax
from jax.experimental import pallas as pl
from jax.experimental.pallas import tpu as pltpu
from jax.sharding import PartitionSpec as P

F32 = jnp.float32
BF16 = jnp.bfloat16
HIGHEST = lax.Precision.HIGHEST
CHUNK = 8
PANEL = 32
MIB = 1024 * 1024


def vmem():
    return pl.BlockSpec(memory_space=pltpu.VMEM)


def smem():
    return pl.BlockSpec(memory_space=pltpu.SMEM)


def params(mib):
    return pltpu.CompilerParams(vmem_limit_bytes=mib * MIB)


def cost(flops, size):
    return pl.CostEstimate(flops=flops, bytes_accessed=size, transcendentals=0)


def times_transposed(a, b, precision=None):
    return lax.dot_general(
        a, b, (((1,), (1,)), ((), ())), precision=precision, preferred_element_type=F32
    )


def transposed_times(a, b):
    return lax.dot_general(a, b, (((0,), (0,)), ((), ())), preferred_element_type=F32)


def slot_column(slot, chips, own):
    return own ^ (2 * (slot % chips) + slot // chips)


def swap(x, axis, size, mask):
    return lax.ppermute(x, axis, [(i, i ^ mask) for i in range(size)])


def gather_columns(x, col_count):
    chips = col_count // 2
    same = [x] + [swap(x, "col", col_count, 2 * m) for m in range(1, chips)]
    return same + [swap(y, "col", col_count, 1) for y in same]


def halves_kernel(own, other, after, *outs):
    del after
    for m, out in enumerate(outs):
        out[...] = own[m] + other[m]


def scatter_sum(other_half, own_half, after, col_count):
    chips, *shape = own_half.shape
    swapped = swap(other_half, "col", col_count, 1)
    halves = pl.pallas_call(
        halves_kernel,
        in_specs=[vmem(), vmem(), pl.BlockSpec(memory_space=pl.ANY)],
        out_specs=[vmem()] * chips,
        out_shape=[jax.ShapeDtypeStruct(shape, F32)] * chips,
        compiler_params=params(12 * own_half.size // MIB + 4),
        cost_estimate=cost(own_half.size, 12 * own_half.size),
        name="halves",
    )(own_half, swapped, after)
    whole = halves[0]
    for m in range(1, chips):
        whole = whole + swap(halves[m], "col", col_count, 2 * m)
    return whole, halves[0]


class Tables:
    def __init__(self, sections, col_count, blocks):
        self.sections, self.col_count, self.blocks = sections, col_count, blocks
        grid, kids = sections * sections, sections * col_count
        self.starts = {"mine": 0, "roots": grid}
        self.starts["picks"] = self.starts["roots"] + grid
        self.starts["ahead"] = self.starts["picks"] + grid
        self.starts["keep"] = self.starts["ahead"] + kids * sections
        self.starts["into"] = self.starts["keep"] + kids * blocks
        self.size = self.starts["into"] + kids * blocks

    def at(self, name, s, *rest):
        place = s
        widths = {"ahead": (self.col_count, self.sections)}.get(name, (self.col_count, self.blocks))
        if name in ("mine", "roots", "picks"):
            widths = (self.sections,)
        for index, width in zip(rest, widths):
            place = place * width + index
        return self.starts[name] + place


def tables_kernel(layout, place, diag, parent, chain, out):
    sections, col_count, local_blocks = layout.sections, layout.col_count, layout.blocks
    chips = col_count // 2
    own = place[0]
    row = place[1]

    def path(s, column):
        columns = [column]
        for t in range(s, sections - 1):
            columns.append(parent[t, columns[-1]])
        return columns

    def block_of(s, columns, j):
        if j == 0:
            return jnp.int32(0)
        if j == 1:
            return jnp.int32(1)
        wanted = block_of(s + 1, columns[1:], j - 1)
        group = diag[s + j, columns[j]]
        found = jnp.int32(0)
        for q in range(1, local_blocks):
            found = jnp.where(chain[group, s, columns[0], q] == wanted, q, found)
        return found

    for s in range(sections):
        columns = path(s, own)
        for j in range(sections - s):
            group = diag[s + j, columns[j]]
            out[layout.at("mine", s, j)] = jnp.where(group == row, 1, 0)
            out[layout.at("roots", s, j)] = group
            out[layout.at("picks", s, j)] = block_of(s, columns, j)
    for s in range(1, sections):
        for slot in range(col_count):
            child = slot_column(slot, chips, own)
            hit = parent[s - 1, child] == own
            columns = path(s - 1, child)
            for j in range(sections - s):
                block = block_of(s - 1, columns, j + 1)
                group = diag[s + j, columns[j + 1]]
                left_out = (block == 0) & (group == diag[s - 1, child])
                out[layout.at("ahead", s, slot, j)] = jnp.where(
                    hit & jnp.logical_not(left_out), 1, 0
                )
            for q in range(local_blocks):
                left_out = (diag[s - 1, child] == row) & (q == 0)
                out[layout.at("keep", s, slot, q)] = jnp.where(
                    hit & jnp.logical_not(left_out), 1, 0
                )
                out[layout.at("into", s, slot, q)] = chain[row, s - 1, child, q]


def pick_kernel(index, source, out):
    for i in range(out.shape[0]):
        out[i] = source[index[i]]


def pick(source, index, block, rows):
    count, width = index.shape[0], source.shape[2]
    return pl.pallas_call(
        pick_kernel,
        grid_spec=pltpu.PrefetchScalarGridSpec(
            num_scalar_prefetch=1,
            grid=(1,),
            in_specs=[pl.BlockSpec((source.shape[0], rows, width), lambda g, a: (0, block, 0))],
            out_specs=pl.BlockSpec((count, rows, width), lambda g, a: (0, 0, 0)),
        ),
        out_shape=jax.ShapeDtypeStruct((count, rows, width), source.dtype),
        compiler_params=params(48),
        cost_estimate=cost(0, 4 * count * rows * width),
        name="pick",
    )(index, source)


def sum_kernel(after, x, out):
    del after
    total = x[0]
    for r in range(1, x.shape[0]):
        total = total + x[r]
    out[...] = total


def sum_rows(x, after):
    return pl.pallas_call(
        sum_kernel,
        in_specs=[pl.BlockSpec(memory_space=pl.ANY), vmem()],
        out_specs=vmem(),
        out_shape=jax.ShapeDtypeStruct(x.shape[1:], x.dtype),
        compiler_params=params(8),
        cost_estimate=cost(x.size, 4 * x.size),
        name="sum_rows",
    )(after, x)


def diagonal_kernel(table, heads, other, own, total):
    g = pl.program_id(0)
    chips = own.shape[0]
    sections = table.shape[0]

    @pl.when(g == 0)
    def _():
        total[...] = jnp.zeros_like(total)

    for t in range(heads.shape[0]):
        product = times_transposed(heads[t], heads[t])
        for s in range(sections):
            total[table[s, 0, g * heads.shape[0] + t], s] += product

    @pl.when(g == pl.num_programs(0) - 1)
    def _():
        own[...] = total[:chips]
        other[...] = total[chips : 2 * chips]


def diagonal_sums(table, heads, chips):
    count, width, _ = heads.shape
    sections = table.shape[0]
    chunk = min(CHUNK, count)
    half = (chips, sections, width, width)
    out = jax.ShapeDtypeStruct(half, F32)
    return pl.pallas_call(
        diagonal_kernel,
        grid_spec=pltpu.PrefetchScalarGridSpec(
            num_scalar_prefetch=1,
            grid=(count // chunk,),
            in_specs=[pl.BlockSpec((chunk, width, width), lambda g, a: (g, 0, 0))],
            out_specs=[pl.BlockSpec(half, lambda g, a: (0, 0, 0, 0))] * 2,
            scratch_shapes=[pltpu.VMEM((2 * chips + 1,) + half[1:], F32)],
        ),
        out_shape=[out, out],
        compiler_params=params(6 * chips * sections * width * width * 4 // MIB + 8),
        cost_estimate=cost(count * width * width * width * 4, count * width * width * 4),
        name="diagonal_sums",
    )(table, heads)


def source_kernel(soon, table, first, second, heads, after, other, own, *refs):
    del after
    rest, total = refs[:-1], refs[-1]
    g = pl.program_id(0)
    chunk, width, _ = first.shape
    chips = own.shape[0]
    blocks = second.shape[1] + 1
    sections = table.shape[0]

    @pl.when(g == 0)
    def _():
        total[...] = jnp.zeros_like(total)

    for t in range(chunk):
        i = g * chunk + t
        panel = jnp.concatenate([first[t]] + [second[t, q] for q in range(blocks - 1)], axis=0)
        for begin in range(0, sections, 2):
            steps = range(begin, min(begin + 2, sections))
            stacked = jnp.concatenate([heads[table[s, 1, i], t] for s in steps], axis=0)
            product = times_transposed(panel, stacked)
            for k, s in enumerate(steps):
                slot = table[s, 0, i]
                for q in range(blocks):
                    total[slot, s * blocks + table[s, 2 + q, i]] += product[
                        q * width : (q + 1) * width, k * width : (k + 1) * width
                    ]

    @pl.when(g == pl.num_programs(0) - 1)
    def _():
        other[...] = total[chips : 2 * chips, : soon * blocks]
        own[...] = total[:chips, : soon * blocks]
        if rest:
            rest[0][...] = total[chips : 2 * chips, soon * blocks :]
            rest[1][...] = total[:chips, soon * blocks :]


def source_sums(soon, table, first, second, heads, after, chips):
    count, width, _ = first.shape
    blocks = 1 + second.shape[1]
    sections = table.shape[0]
    chunk = min(CHUNK, count)
    shapes = [(chips, soon * blocks, width, width)] * 2
    if soon < sections:
        shapes += [(chips, (sections - soon) * blocks, width, width)] * 2
    size = 4 * chips * sections * blocks * width * width
    return pl.pallas_call(
        functools.partial(source_kernel, soon),
        grid_spec=pltpu.PrefetchScalarGridSpec(
            num_scalar_prefetch=1,
            grid=(count // chunk,),
            in_specs=[
                pl.BlockSpec((chunk, width, width), lambda g, a: (g, 0, 0)),
                pl.BlockSpec((chunk, blocks - 1, width, width), lambda g, a: (g, 0, 0, 0)),
                pl.BlockSpec((heads.shape[0], chunk, width, width), lambda g, a: (0, g, 0, 0)),
                pl.BlockSpec(memory_space=pl.ANY),
            ],
            out_specs=[pl.BlockSpec(shape, lambda g, a: (0, 0, 0, 0)) for shape in shapes],
            scratch_shapes=[pltpu.VMEM((2 * chips, sections * blocks, width, width), F32)],
        ),
        out_shape=[jax.ShapeDtypeStruct(shape, F32) for shape in shapes],
        compiler_params=params(6 * size // MIB + 26),
        cost_estimate=cost(
            count * blocks * width * width * width * 2 * sections, count * width * width * 12
        ),
        name="source_sums",
    )(table, first, second, heads, after)


def known_kernel(layout, begin, steps, pairs, tables, after, targets, sums, *refs):
    del after
    starts, out = refs[:-1], refs[-1]
    zeros = jnp.zeros(out.shape[1:], F32)
    n = 0
    for s, j in pairs:
        block = starts[0][s - begin, tables[layout.at("picks", s, j)]]
        out[n] = jnp.where(tables[layout.at("mine", s, j)] > 0, block, zeros)
        n += 1
    for s in steps:
        block = targets[s, 0] - sums[s]
        out[n] = jnp.where(tables[layout.at("mine", s, 0)] > 0, block, zeros)
        n += 1


def known_blocks(
    layout, steps, pairs, tables, after, targets, sums, starts=None, begin=0
):
    width = targets.shape[-1]
    arrays = [targets, sums] + ([] if starts is None else [starts])
    shape = (len(steps) + len(pairs), width, width)
    return pl.pallas_call(
        functools.partial(known_kernel, layout, begin, steps, pairs),
        in_specs=[smem(), pl.BlockSpec(memory_space=pl.ANY)] + [vmem()] * len(arrays),
        out_specs=vmem(),
        out_shape=jax.ShapeDtypeStruct(shape, F32),
        compiler_params=params(8),
        cost_estimate=cost(targets.size, 4 * targets.size),
        name="known_blocks",
    )(tables, after, *arrays)


def message_kernel(layout, tables, whole, own, out):
    ahead = layout.sections - 1
    for j in range(ahead):
        group = tables[layout.at("roots", 0, j + 1)]
        out[j] = whole[group, tables[layout.at("picks", 0, j + 1)]]
    out[ahead:] = own[...]


def first_message(layout, tables, whole, own):
    blocks, width, _ = own.shape
    shape = (layout.sections - 1 + blocks, width, width)
    return pl.pallas_call(
        functools.partial(message_kernel, layout),
        in_specs=[smem(), vmem(), vmem()],
        out_specs=vmem(),
        out_shape=jax.ShapeDtypeStruct(shape, own.dtype),
        compiler_params=params(4),
        cost_estimate=cost(own.size, 8 * own.size),
        name="first_message",
    )(tables, whole, own)


def split(x):
    high = x.astype(BF16)
    rest = x - high.astype(F32)
    middle = rest.astype(BF16)
    low = (rest - middle.astype(F32)).astype(BF16)
    return high, middle, low


def factor_kernel(step, layout, tables, start, *refs):
    children, (upper, inverse, work) = refs[:-3], refs[-3:]
    width = start.shape[0]
    work[:, :width] = start[...]
    for slot, child in enumerate(children):

        @pl.when(tables[layout.at("ahead", step, slot, 0)] > 0)
        def _(child=child):
            work[:, :width] -= times_transposed(child[0], child[0])

    rows = lax.broadcasted_iota(jnp.int32, (width, width), 0)
    columns = lax.broadcasted_iota(jnp.int32, (width, width), 1)
    work[:, width:] = (rows == columns).astype(F32)
    sub = lax.broadcasted_iota(jnp.int32, (PANEL, 1), 0)
    for first in range(0, width, PANEL):
        last = first + PANEL
        slab = work[first:last, :]
        spans = [
            jnp.broadcast_to(slab[:, first + k : first + k + 1], (PANEL, width))
            for k in range(PANEL)
        ]
        scale = jnp.zeros((PANEL, 1), F32)
        for j in range(PANEL):
            pivot = spans[j][j : j + 1, :]
            ratio = jnp.where(sub > j, spans[j] * (1.0 / pivot), 0.0)
            for k in range(j + 1, PANEL):
                spans[k] = spans[k] - ratio * spans[k][j : j + 1, :]
            slab = slab - jnp.concatenate([ratio, ratio], axis=1) * slab[j : j + 1, :]
            scale = jnp.where(sub == j, lax.rsqrt(pivot[:, 0:1]), scale)
        slab = slab * scale
        work[first:last, :] = slab
        if last < width:
            high, middle, low = split(slab)
            left = jnp.concatenate([high, high, middle, middle, high, low], axis=0)
            right = jnp.concatenate([high, middle, high, middle, low, high], axis=0)
            work[last:, :] = work[last:, :] - transposed_times(left[:, last:width], right)
    upper[...] = jnp.where(rows <= columns, work[:, :width], 0.0)
    inverse[...] = work[:, width:]


def factor(step, layout, tables, start, children):
    width = start.shape[0]
    out = jax.ShapeDtypeStruct((width, width), F32)
    return pl.pallas_call(
        functools.partial(factor_kernel, step, layout),
        in_specs=[smem(), vmem()] + [vmem()] * len(children),
        out_specs=[vmem(), vmem()],
        out_shape=[out, out],
        scratch_shapes=[pltpu.VMEM((width, 2 * width), F32)],
        compiler_params=params(8),
        cost_estimate=cost(width * width * width * 200, 16 * width * width),
        name="factor",
    )(tables, start, *children)


def blocks_kernel(step, layout, ahead, send, tables, after, start, inverse, upper, *refs):
    del after
    work, refs = refs[-1], refs[:-1]
    rounded, refs = (refs[-1], refs[:-1]) if send else (None, refs)
    out, refs = refs[-1], refs[:-1]
    later, children = (refs[0], refs[1:]) if ahead else (None, refs)
    blocks, width = start.shape[0], start.shape[1]
    for j in range(ahead):
        work[j] = later[j]
    work[ahead:] = start[...]
    for slot, child in enumerate(children):
        skipped = child.shape[0] - blocks
        for j in range(ahead):

            @pl.when(tables[layout.at("ahead", step, slot, j + 1)] > 0)
            def _(slot=slot, child=child, j=j):
                work[j] -= times_transposed(child[j + 1], child[0])

        for q in range(blocks):

            @pl.when(tables[layout.at("keep", step, slot, q)] > 0)
            def _(slot=slot, child=child, q=q):
                into = tables[layout.at("into", step, slot, q)]
                work[ahead + into] -= times_transposed(child[skipped + q], child[0])

    solved = times_transposed(
        work[...].reshape((ahead + blocks) * width, width), inverse[...], HIGHEST
    )
    out[...] = solved[ahead * width :]
    if send:
        rounded[...] = solved.astype(BF16).reshape(ahead + blocks, width, width)

    @pl.when(tables[layout.at("mine", step, 0)] > 0)
    def _():
        out[:width, :] = upper[...].T


def panel_blocks(step, layout, tables, after, start, later, send, inverse, upper, children):
    blocks, width, _ = start.shape
    ahead = 0 if later is None else later.shape[0]
    arrays = [start, inverse, upper] + ([later] if ahead else []) + list(children)
    out = [jax.ShapeDtypeStruct((blocks * width, width), F32)]
    if send:
        out.append(jax.ShapeDtypeStruct((ahead + blocks, width, width), BF16))
    return pl.pallas_call(
        functools.partial(blocks_kernel, step, layout, ahead, send),
        in_specs=[smem(), pl.BlockSpec(memory_space=pl.ANY)] + [vmem()] * len(arrays),
        out_specs=[vmem()] * len(out),
        out_shape=out,
        scratch_shapes=[pltpu.VMEM((blocks + ahead, width, width), F32)],
        compiler_params=params(12),
        cost_estimate=cost(start.size * 2000, start.size * 16),
        name="panel_blocks",
    )(tables, after, *arrays)


def local(targets, src_panels, live_counts, dest_owner, relative_map, diag_row, parent, chain_map):
    col_count = lax.axis_size("col")
    row_count = lax.axis_size("row")
    own = lax.axis_index("col")
    row_index = lax.axis_index("row")
    chips = col_count // 2
    src_count, _, width = src_panels.shape
    local_blocks = src_panels.shape[1] // width
    sections = targets.shape[0]
    targets = targets.reshape(sections, local_blocks, width, width)

    place = jnp.stack([own, row_index]).astype(jnp.int32)

    dealt = src_count // 2
    share = src_count // col_count
    facts = jnp.concatenate(
        [
            dest_owner.T,
            relative_map.transpose(1, 2, 0).reshape(sections * local_blocks, src_count),
            jnp.broadcast_to(live_counts, (1, src_count)),
        ],
        axis=0,
    ).astype(jnp.int32)
    facts = lax.all_gather(facts, "col", axis=0)
    counts = facts[:, -1, 0]
    columns_of = jnp.arange(col_count)
    offsets = jnp.sum(jnp.where(columns_of[None, :] < columns_of[:, None], counts[None, :], 0), axis=1)
    own_offset = jnp.sum(jnp.where(columns_of == own, offsets, 0))
    sent = (
        jnp.mod(columns_of - own_offset, col_count)[:, None]
        + col_count * jnp.arange(share)[None, :]
    ).reshape(-1)
    number = jnp.arange(dealt) * col_count + own
    source_column = jnp.sum(
        (offsets[None, :] <= number[:, None]).astype(jnp.int32), axis=1
    ) - 1
    index = number - jnp.sum(
        jnp.where(columns_of[None, :] == source_column[:, None], offsets[None, :], 0), axis=1
    )
    kept = source_column * share + index // col_count

    def deal(block):
        mixed = lax.all_to_all(pick(src_panels, sent, block, width), "col", 0, 0, tiled=True)
        return pick(mixed, kept, 0, width)

    first = deal(0)
    heads = lax.all_gather(first, "row", axis=0)
    second = jnp.stack([deal(q) for q in range(1, local_blocks)], axis=1)

    chain = lax.all_gather(chain_map[None], "row", axis=0, tiled=True)
    layout = Tables(sections, col_count, local_blocks)
    tables = pl.pallas_call(
        functools.partial(tables_kernel, layout),
        in_specs=[smem()] * 4,
        out_specs=smem(),
        out_shape=jax.ShapeDtypeStruct((layout.size,), jnp.int32),
        name="tables",
    )(place, diag_row, parent, chain)

    facts = facts.transpose(0, 2, 1).reshape(col_count * src_count, -1)
    facts = facts[source_column * src_count + index]
    dest = facts[:, :sections].T
    target_blocks = facts[:, sections:-1].T.reshape(sections, local_blocks, dealt)
    offset = jnp.bitwise_xor(dest, own)
    slots = (offset % 2) * chips + offset // 2
    source_root = jnp.sum(
        jnp.where(dest[:, :, None] == columns_of, diag_row[:, None, :], 0), axis=-1
    )
    table = jnp.concatenate([slots[:, None], source_root[:, None], target_blocks], axis=1)
    held = jnp.where(source_root == row_index, slots, 2 * chips)[:, None]

    other, mine = diagonal_sums(held, first, chips)
    total, _ = scatter_sum(other, mine, place, col_count)

    def share(x):
        return jnp.sum(lax.all_gather(x, "row", axis=0), axis=0)

    last = sections - 1
    soon = min(2, sections)
    diagonals = share(known_blocks(layout, [0], [], tables, place, targets, total))
    diagonals = [diagonals[0]]
    factored = factor(0, layout, tables, diagonals[0], [])

    sums = source_sums(soon, table, first, second, heads, factored[0], chips)
    whole, _ = scatter_sum(sums[0], sums[1], place, col_count)
    early = targets[:soon] - whole.reshape(targets[:soon].shape)
    starts = [early[s] for s in range(soon)]
    sent_rest = place
    if soon < sections:
        whole, sent_rest = scatter_sum(sums[2], sums[3], whole, col_count)
        late = targets[soon:] - whole.reshape(targets[soon:].shape)
        starts += [late[s - soon] for s in range(soon, sections)]

    later = [None] * sections
    pairs = [(s, j) for s in range(1, min(soon, last)) for j in range(1, sections - s)]
    middle = range(1, min(soon + 1, sections))
    if last:
        group = known_blocks(layout, middle, pairs, tables, place, targets, total, early)
        whole = sum_rows(lax.all_gather(group, "row", axis=0), place)
        if pairs:
            later[1] = whole[: len(pairs)]
        diagonals += [whole[len(pairs) + n] for n in range(len(middle))]

    results, children = [], []
    for s in range(sections):
        upper, inverse = factored
        if s > 0:
            upper, inverse = factor(s, layout, tables, diagonals[s], children)
        if s == soon and s < last:
            spread = sum_rows(gathered, upper)
            diagonals += [spread[len(padded) + n] for n in range(len(final))]
            for t in range(soon, last):
                at = pairs.index((t, 1))
                later[t] = spread[at : at + last - t]
        made = panel_blocks(
            s, layout, tables, sent_rest if s == 0 else place, starts[s],
            later[s], s < last, inverse, upper, children
        )
        results.append(made[0])
        if s < last:
            message = made[1]
            if s == 0:
                whole = lax.all_gather(message, "row", axis=0)
                message = first_message(layout, tables, whole, message)
                pairs = [(t, j) for t in range(soon, last) for j in range(1, sections - t)]
                final = range(len(diagonals), sections)
                if pairs:
                    padded = pairs + pairs[:1] * (4 - len(pairs) - len(final))
                    known = known_blocks(
                        layout, final, padded, tables, whole, targets, total, late, soon
                    )
                    gathered = lax.all_gather(known, "row", axis=0)
            children = gather_columns(message, col_count)
    return jnp.stack(results)[:, None]


def solution(mesh):
    return jax.shard_map(
        local,
        mesh=mesh,
        in_specs=(
            P(None, "col", "row", None),
            P("col", "row", None),
            P("col"),
            P("col", None),
            P("col", None, "row"),
            P(),
            P(),
            P(None, None, "row"),
        ),
        out_specs=P(None, "col", "row", None),
        check_vma=False,
    )
```

```python
import functools

import jax
import jax.numpy as jnp
from jax import lax
from jax.experimental import pallas as pl
from jax.experimental.pallas import tpu as pltpu
from jax.sharding import PartitionSpec as P

F32 = jnp.float32
BF16 = jnp.bfloat16
HIGHEST = lax.Precision.HIGHEST
CHUNK = 8
PANEL = 32
MIB = 1024 * 1024


def vmem():
    return pl.BlockSpec(memory_space=pltpu.VMEM)


def smem():
    return pl.BlockSpec(memory_space=pltpu.SMEM)


def params(mib):
    return pltpu.CompilerParams(vmem_limit_bytes=mib * MIB)


def cost(flops, size):
    return pl.CostEstimate(flops=flops, bytes_accessed=size, transcendentals=0)


def times_transposed(a, b, precision=None):
    return lax.dot_general(
        a, b, (((1,), (1,)), ((), ())), precision=precision, preferred_element_type=F32
    )


def transposed_times(a, b):
    return lax.dot_general(a, b, (((0,), (0,)), ((), ())), preferred_element_type=F32)


def slot_column(slot, chips, own):
    return own ^ (2 * (slot % chips) + slot // chips)


def swap(x, axis, size, mask):
    return lax.ppermute(x, axis, [(i, i ^ mask) for i in range(size)])


def gather_columns(x, col_count):
    chips = col_count // 2
    same = [x] + [swap(x, "col", col_count, 2 * m) for m in range(1, chips)]
    return same + [swap(y, "col", col_count, 1) for y in same]


def halves_kernel(own, other, after, *outs):
    del after
    for m, out in enumerate(outs):
        out[...] = own[m] + other[m]


def scatter_sum(other_half, own_half, after, col_count):
    chips, *shape = own_half.shape
    swapped = swap(other_half, "col", col_count, 1)
    halves = pl.pallas_call(
        halves_kernel,
        in_specs=[vmem(), vmem(), pl.BlockSpec(memory_space=pl.ANY)],
        out_specs=[vmem()] * chips,
        out_shape=[jax.ShapeDtypeStruct(shape, F32)] * chips,
        compiler_params=params(12 * own_half.size // MIB + 4),
        cost_estimate=cost(own_half.size, 12 * own_half.size),
        name="halves",
    )(own_half, swapped, after)
    whole = halves[0]
    for m in range(1, chips):
        whole = whole + swap(halves[m], "col", col_count, 2 * m)
    return whole, halves[0]


class Tables:
    def __init__(self, sections, col_count, blocks):
        self.sections, self.col_count, self.blocks = sections, col_count, blocks
        grid, kids = sections * sections, sections * col_count
        self.starts = {"mine": 0, "roots": grid}
        self.starts["picks"] = self.starts["roots"] + grid
        self.starts["ahead"] = self.starts["picks"] + grid
        self.starts["keep"] = self.starts["ahead"] + kids * sections
        self.starts["into"] = self.starts["keep"] + kids * blocks
        self.size = self.starts["into"] + kids * blocks

    def at(self, name, s, *rest):
        place = s
        widths = {"ahead": (self.col_count, self.sections)}.get(name, (self.col_count, self.blocks))
        if name in ("mine", "roots", "picks"):
            widths = (self.sections,)
        for index, width in zip(rest, widths):
            place = place * width + index
        return self.starts[name] + place


def tables_kernel(layout, place, diag, parent, chain, out):
    sections, col_count, local_blocks = layout.sections, layout.col_count, layout.blocks
    chips = col_count // 2
    own = place[0]
    row = place[1]

    def path(s, column):
        columns = [column]
        for t in range(s, sections - 1):
            columns.append(parent[t, columns[-1]])
        return columns

    def block_of(s, columns, j):
        if j == 0:
            return jnp.int32(0)
        if j == 1:
            return jnp.int32(1)
        wanted = block_of(s + 1, columns[1:], j - 1)
        group = diag[s + j, columns[j]]
        found = jnp.int32(0)
        for q in range(1, local_blocks):
            found = jnp.where(chain[group, s, columns[0], q] == wanted, q, found)
        return found

    for s in range(sections):
        columns = path(s, own)
        for j in range(sections - s):
            group = diag[s + j, columns[j]]
            out[layout.at("mine", s, j)] = jnp.where(group == row, 1, 0)
            out[layout.at("roots", s, j)] = group
            out[layout.at("picks", s, j)] = block_of(s, columns, j)
    for s in range(1, sections):
        for slot in range(col_count):
            child = slot_column(slot, chips, own)
            hit = parent[s - 1, child] == own
            columns = path(s - 1, child)
            for j in range(sections - s):
                block = block_of(s - 1, columns, j + 1)
                group = diag[s + j, columns[j + 1]]
                left_out = (block == 0) & (group == diag[s - 1, child])
                out[layout.at("ahead", s, slot, j)] = jnp.where(
                    hit & jnp.logical_not(left_out), 1, 0
                )
            for q in range(local_blocks):
                left_out = (diag[s - 1, child] == row) & (q == 0)
                out[layout.at("keep", s, slot, q)] = jnp.where(
                    hit & jnp.logical_not(left_out), 1, 0
                )
                out[layout.at("into", s, slot, q)] = chain[row, s - 1, child, q]


def split_kernel(index, source, *outs):
    share = outs[0].shape[0]
    for k, out in enumerate(outs):
        for m in range(share):
            out[m] = source[index[k * share + m]]


def split_panels(source, index, block, width, parts):
    share = index.shape[0] // parts
    shape = (share, width, source.shape[2])
    return pl.pallas_call(
        split_kernel,
        grid_spec=pltpu.PrefetchScalarGridSpec(
            num_scalar_prefetch=1,
            grid=(1,),
            in_specs=[
                pl.BlockSpec((source.shape[0], width, source.shape[2]), lambda g, a: (0, block, 0))
            ],
            out_specs=[pl.BlockSpec(shape, lambda g, a: (0, 0, 0))] * parts,
        ),
        out_shape=[jax.ShapeDtypeStruct(shape, source.dtype)] * parts,
        compiler_params=params(48),
        cost_estimate=cost(0, 4 * index.shape[0] * width * source.shape[2]),
        name="split_panels",
    )(index, source)


def merge_kernel(index, *refs):
    parts, (out, work) = refs[:-2], refs[-2:]
    share = parts[0].shape[0]
    for k, part in enumerate(parts):
        work[k * share : (k + 1) * share] = part[...]
    for i in range(out.shape[0]):
        out[i] = work[index[i]]


def merge_panels(parts, index):
    share, width, _ = parts[0].shape
    count = index.shape[0]
    return pl.pallas_call(
        merge_kernel,
        in_specs=[smem()] + [vmem()] * len(parts),
        out_specs=vmem(),
        out_shape=jax.ShapeDtypeStruct((count,) + parts[0].shape[1:], parts[0].dtype),
        scratch_shapes=[pltpu.VMEM((len(parts) * share,) + parts[0].shape[1:], parts[0].dtype)],
        compiler_params=params(16),
        cost_estimate=cost(0, 8 * count * width * width),
        name="merge_panels",
    )(index, *parts)


def sum_kernel(after, x, out):
    del after
    total = x[0]
    for r in range(1, x.shape[0]):
        total = total + x[r]
    out[...] = total


def sum_rows(x, after):
    return pl.pallas_call(
        sum_kernel,
        in_specs=[pl.BlockSpec(memory_space=pl.ANY), vmem()],
        out_specs=vmem(),
        out_shape=jax.ShapeDtypeStruct(x.shape[1:], x.dtype),
        compiler_params=params(8),
        cost_estimate=cost(x.size, 4 * x.size),
        name="sum_rows",
    )(after, x)


def diagonal_kernel(table, heads, other, own, total):
    g = pl.program_id(0)
    chips = own.shape[0]
    sections = table.shape[0]

    @pl.when(g == 0)
    def _():
        total[...] = jnp.zeros_like(total)

    for t in range(heads.shape[0]):
        product = times_transposed(heads[t], heads[t])
        for s in range(sections):
            total[table[s, 0, g * heads.shape[0] + t], s] += product

    @pl.when(g == pl.num_programs(0) - 1)
    def _():
        own[...] = total[:chips]
        other[...] = total[chips : 2 * chips]


def diagonal_sums(table, heads, chips):
    count, width, _ = heads.shape
    sections = table.shape[0]
    chunk = min(CHUNK, count)
    half = (chips, sections, width, width)
    out = jax.ShapeDtypeStruct(half, F32)
    return pl.pallas_call(
        diagonal_kernel,
        grid_spec=pltpu.PrefetchScalarGridSpec(
            num_scalar_prefetch=1,
            grid=(count // chunk,),
            in_specs=[pl.BlockSpec((chunk, width, width), lambda g, a: (g, 0, 0))],
            out_specs=[pl.BlockSpec(half, lambda g, a: (0, 0, 0, 0))] * 2,
            scratch_shapes=[pltpu.VMEM((2 * chips + 1,) + half[1:], F32)],
        ),
        out_shape=[out, out],
        compiler_params=params(6 * chips * sections * width * width * 4 // MIB + 8),
        cost_estimate=cost(count * width * width * width * 4, count * width * width * 4),
        name="diagonal_sums",
    )(table, heads)


def source_kernel(soon, table, first, second, heads, after, other, own, *refs):
    del after
    rest, total = refs[:-1], refs[-1]
    g = pl.program_id(0)
    chunk, width, _ = first.shape
    chips = own.shape[0]
    blocks = second.shape[1] + 1
    sections = table.shape[0]

    @pl.when(g == 0)
    def _():
        total[...] = jnp.zeros_like(total)

    for t in range(chunk):
        i = g * chunk + t
        panel = jnp.concatenate([first[t]] + [second[t, q] for q in range(blocks - 1)], axis=0)
        for begin in range(0, sections, 2):
            steps = range(begin, min(begin + 2, sections))
            stacked = jnp.concatenate([heads[table[s, 1, i], t] for s in steps], axis=0)
            product = times_transposed(panel, stacked)
            for k, s in enumerate(steps):
                slot = table[s, 0, i]
                for q in range(blocks):
                    total[slot, s * blocks + table[s, 2 + q, i]] += product[
                        q * width : (q + 1) * width, k * width : (k + 1) * width
                    ]

    @pl.when(g == pl.num_programs(0) - 1)
    def _():
        other[...] = total[chips : 2 * chips, : soon * blocks]
        own[...] = total[:chips, : soon * blocks]
        if rest:
            rest[0][...] = total[chips : 2 * chips, soon * blocks :]
            rest[1][...] = total[:chips, soon * blocks :]


def source_sums(soon, table, first, second, heads, after, chips):
    count, width, _ = first.shape
    blocks = 1 + second.shape[1]
    sections = table.shape[0]
    chunk = min(CHUNK, count)
    shapes = [(chips, soon * blocks, width, width)] * 2
    if soon < sections:
        shapes += [(chips, (sections - soon) * blocks, width, width)] * 2
    size = 4 * chips * sections * blocks * width * width
    return pl.pallas_call(
        functools.partial(source_kernel, soon),
        grid_spec=pltpu.PrefetchScalarGridSpec(
            num_scalar_prefetch=1,
            grid=(count // chunk,),
            in_specs=[
                pl.BlockSpec((chunk, width, width), lambda g, a: (g, 0, 0)),
                pl.BlockSpec((chunk, blocks - 1, width, width), lambda g, a: (g, 0, 0, 0)),
                pl.BlockSpec((heads.shape[0], chunk, width, width), lambda g, a: (0, g, 0, 0)),
                pl.BlockSpec(memory_space=pl.ANY),
            ],
            out_specs=[pl.BlockSpec(shape, lambda g, a: (0, 0, 0, 0)) for shape in shapes],
            scratch_shapes=[pltpu.VMEM((2 * chips, sections * blocks, width, width), F32)],
        ),
        out_shape=[jax.ShapeDtypeStruct(shape, F32) for shape in shapes],
        compiler_params=params(6 * size // MIB + 26),
        cost_estimate=cost(
            count * blocks * width * width * width * 2 * sections, count * width * width * 12
        ),
        name="source_sums",
    )(table, first, second, heads, after)


def known_kernel(layout, begin, steps, pairs, tables, after, targets, sums, *refs):
    del after
    starts, out = refs[:-1], refs[-1]
    zeros = jnp.zeros(out.shape[1:], F32)
    n = 0
    for s, j in pairs:
        block = starts[0][s - begin, tables[layout.at("picks", s, j)]]
        out[n] = jnp.where(tables[layout.at("mine", s, j)] > 0, block, zeros)
        n += 1
    for s in steps:
        block = targets[s, 0] - sums[s]
        out[n] = jnp.where(tables[layout.at("mine", s, 0)] > 0, block, zeros)
        n += 1


def known_blocks(
    layout, steps, pairs, tables, after, targets, sums, starts=None, begin=0
):
    width = targets.shape[-1]
    arrays = [targets, sums] + ([] if starts is None else [starts])
    shape = (len(steps) + len(pairs), width, width)
    return pl.pallas_call(
        functools.partial(known_kernel, layout, begin, steps, pairs),
        in_specs=[smem(), pl.BlockSpec(memory_space=pl.ANY)] + [vmem()] * len(arrays),
        out_specs=vmem(),
        out_shape=jax.ShapeDtypeStruct(shape, F32),
        compiler_params=params(8),
        cost_estimate=cost(targets.size, 4 * targets.size),
        name="known_blocks",
    )(tables, after, *arrays)


def message_kernel(layout, tables, whole, own, out):
    ahead = layout.sections - 1
    for j in range(ahead):
        group = tables[layout.at("roots", 0, j + 1)]
        out[j] = whole[group, tables[layout.at("picks", 0, j + 1)]]
    out[ahead:] = own[...]


def first_message(layout, tables, whole, own):
    blocks, width, _ = own.shape
    shape = (layout.sections - 1 + blocks, width, width)
    return pl.pallas_call(
        functools.partial(message_kernel, layout),
        in_specs=[smem(), vmem(), vmem()],
        out_specs=vmem(),
        out_shape=jax.ShapeDtypeStruct(shape, own.dtype),
        compiler_params=params(4),
        cost_estimate=cost(own.size, 8 * own.size),
        name="first_message",
    )(tables, whole, own)


def split(x):
    high = x.astype(BF16)
    rest = x - high.astype(F32)
    middle = rest.astype(BF16)
    low = (rest - middle.astype(F32)).astype(BF16)
    return high, middle, low


def factor_kernel(step, layout, tables, start, *refs):
    children, (upper, inverse, work) = refs[:-3], refs[-3:]
    width = start.shape[0]
    work[:, :width] = start[...]
    for slot, child in enumerate(children):

        @pl.when(tables[layout.at("ahead", step, slot, 0)] > 0)
        def _(child=child):
            work[:, :width] -= times_transposed(child[0], child[0])

    rows = lax.broadcasted_iota(jnp.int32, (width, width), 0)
    columns = lax.broadcasted_iota(jnp.int32, (width, width), 1)
    work[:, width:] = (rows == columns).astype(F32)
    groups = range(PANEL // 8)
    sub = lax.broadcasted_iota(jnp.int32, (8, 1), 0)
    for first in range(0, width, PANEL):
        last = first + PANEL
        slab = [work[first + 8 * g : first + 8 * g + 8, :] for g in groups]
        spans = [
            {
                g: jnp.broadcast_to(slab[g][:, first + k : first + k + 1], (8, width))
                for g in groups
                if g >= k // 8
            }
            for k in range(PANEL)
        ]
        scale = [jnp.zeros((8, 1), F32) for _ in groups]
        for j in range(PANEL):
            here, row = divmod(j, 8)
            pivot = spans[j][here][row : row + 1, :]
            inverted = 1.0 / pivot
            ratio = {g: span * inverted for g, span in spans[j].items()}
            ratio[here] = jnp.where(sub > row, ratio[here], 0.0)
            for k in range(j + 1, PANEL):
                crossing = spans[j][k // 8][k % 8 : k % 8 + 1, :]
                for g in spans[k]:
                    spans[k][g] = spans[k][g] - ratio[g] * crossing
            line = slab[here][row : row + 1, :]
            for g in ratio:
                slab[g] = slab[g] - jnp.concatenate([ratio[g], ratio[g]], axis=1) * line
            scale[here] = jnp.where(sub == row, lax.rsqrt(pivot[:, 0:1]), scale[here])
        slab = jnp.concatenate([slab[g] * scale[g] for g in groups], axis=0)
        work[first:last, :] = slab
        if last < width:
            high, middle, low = split(slab)
            left = jnp.concatenate([high, high, middle, middle, high, low], axis=0)
            right = jnp.concatenate([high, middle, high, middle, low, high], axis=0)
            work[last:, :] = work[last:, :] - transposed_times(left[:, last:width], right)
    upper[...] = jnp.where(rows <= columns, work[:, :width], 0.0)
    inverse[...] = work[:, width:]


def factor(step, layout, tables, start, children):
    width = start.shape[0]
    out = jax.ShapeDtypeStruct((width, width), F32)
    return pl.pallas_call(
        functools.partial(factor_kernel, step, layout),
        in_specs=[smem(), vmem()] + [vmem()] * len(children),
        out_specs=[vmem(), vmem()],
        out_shape=[out, out],
        scratch_shapes=[pltpu.VMEM((width, 2 * width), F32)],
        compiler_params=params(8),
        cost_estimate=cost(width * width * width * 200, 16 * width * width),
        name="factor",
    )(tables, start, *children)


def blocks_kernel(step, layout, ahead, send, tables, after, start, inverse, upper, *refs):
    del after
    work, refs = refs[-1], refs[:-1]
    rounded, refs = (refs[-1], refs[:-1]) if send else (None, refs)
    out, refs = refs[-1], refs[:-1]
    later, children = (refs[0], refs[1:]) if ahead else (None, refs)
    blocks, width = start.shape[0], start.shape[1]
    for j in range(ahead):
        work[j] = later[j]
    work[ahead:] = start[...]
    for slot, child in enumerate(children):
        skipped = child.shape[0] - blocks
        for j in range(ahead):

            @pl.when(tables[layout.at("ahead", step, slot, j + 1)] > 0)
            def _(slot=slot, child=child, j=j):
                work[j] -= times_transposed(child[j + 1], child[0])

        for q in range(blocks):

            @pl.when(tables[layout.at("keep", step, slot, q)] > 0)
            def _(slot=slot, child=child, q=q):
                into = tables[layout.at("into", step, slot, q)]
                work[ahead + into] -= times_transposed(child[skipped + q], child[0])

    solved = times_transposed(
        work[...].reshape((ahead + blocks) * width, width), inverse[...], HIGHEST
    )
    out[...] = solved[ahead * width :]
    if send:
        rounded[...] = solved.astype(BF16).reshape(ahead + blocks, width, width)

    @pl.when(tables[layout.at("mine", step, 0)] > 0)
    def _():
        out[:width, :] = upper[...].T


def panel_blocks(step, layout, tables, after, start, later, send, inverse, upper, children):
    blocks, width, _ = start.shape
    ahead = 0 if later is None else later.shape[0]
    arrays = [start, inverse, upper] + ([later] if ahead else []) + list(children)
    out = [jax.ShapeDtypeStruct((blocks * width, width), F32)]
    if send:
        out.append(jax.ShapeDtypeStruct((ahead + blocks, width, width), BF16))
    return pl.pallas_call(
        functools.partial(blocks_kernel, step, layout, ahead, send),
        in_specs=[smem(), pl.BlockSpec(memory_space=pl.ANY)] + [vmem()] * len(arrays),
        out_specs=[vmem()] * len(out),
        out_shape=out,
        scratch_shapes=[pltpu.VMEM((blocks + ahead, width, width), F32)],
        compiler_params=params(12),
        cost_estimate=cost(start.size * 2000, start.size * 16),
        name="panel_blocks",
    )(tables, after, *arrays)


def local(targets, src_panels, live_counts, dest_owner, relative_map, diag_row, parent, chain_map):
    col_count = lax.axis_size("col")
    row_count = lax.axis_size("row")
    own = lax.axis_index("col")
    row_index = lax.axis_index("row")
    chips = col_count // 2
    src_count, _, width = src_panels.shape
    local_blocks = src_panels.shape[1] // width
    sections = targets.shape[0]
    targets = targets.reshape(sections, local_blocks, width, width)

    place = jnp.stack([own, row_index]).astype(jnp.int32)

    dealt = src_count // 2
    share = src_count // col_count
    facts = jnp.concatenate(
        [
            dest_owner.T,
            relative_map.transpose(1, 2, 0).reshape(sections * local_blocks, src_count),
            jnp.broadcast_to(live_counts, (1, src_count)),
        ],
        axis=0,
    ).astype(jnp.int32)
    facts = lax.all_gather(facts, "col", axis=0)
    counts = facts[:, -1, 0]
    columns_of = jnp.arange(col_count)
    offsets = jnp.sum(jnp.where(columns_of[None, :] < columns_of[:, None], counts[None, :], 0), axis=1)
    own_offset = jnp.sum(jnp.where(columns_of == own, offsets, 0))
    partner = jnp.bitwise_xor(columns_of, own)
    sent = (
        jnp.mod(partner - own_offset, col_count)[:, None] + col_count * jnp.arange(share)[None, :]
    ).reshape(-1)
    number = jnp.arange(dealt) * col_count + own
    source_column = jnp.sum(
        (offsets[None, :] <= number[:, None]).astype(jnp.int32), axis=1
    ) - 1
    index = number - jnp.sum(
        jnp.where(columns_of[None, :] == source_column[:, None], offsets[None, :], 0), axis=1
    )
    kept = jnp.bitwise_xor(source_column, own) * share + index // col_count

    def deal(block):
        parts = split_panels(src_panels, sent, block, width, col_count)
        parts = [swap(part, "col", col_count, k) if k else part for k, part in enumerate(parts)]
        return merge_panels(parts, kept)

    first = deal(0)
    heads = lax.all_gather(first, "row", axis=0)
    second = jnp.stack([deal(q) for q in range(1, local_blocks)], axis=1)

    chain = lax.all_gather(chain_map[None], "row", axis=0, tiled=True)
    layout = Tables(sections, col_count, local_blocks)
    tables = pl.pallas_call(
        functools.partial(tables_kernel, layout),
        in_specs=[smem()] * 4,
        out_specs=smem(),
        out_shape=jax.ShapeDtypeStruct((layout.size,), jnp.int32),
        name="tables",
    )(place, diag_row, parent, chain)

    facts = facts.transpose(0, 2, 1).reshape(col_count * src_count, -1)
    facts = facts[source_column * src_count + index]
    dest = facts[:, :sections].T
    target_blocks = facts[:, sections:-1].T.reshape(sections, local_blocks, dealt)
    offset = jnp.bitwise_xor(dest, own)
    slots = (offset % 2) * chips + offset // 2
    source_root = jnp.sum(
        jnp.where(dest[:, :, None] == columns_of, diag_row[:, None, :], 0), axis=-1
    )
    table = jnp.concatenate([slots[:, None], source_root[:, None], target_blocks], axis=1)
    held = jnp.where(source_root == row_index, slots, 2 * chips)[:, None]

    other, mine = diagonal_sums(held, first, chips)
    total, _ = scatter_sum(other, mine, place, col_count)

    def share(x):
        return jnp.sum(lax.all_gather(x, "row", axis=0), axis=0)

    last = sections - 1
    soon = min(2, sections)
    diagonals = share(known_blocks(layout, [0], [], tables, place, targets, total))
    diagonals = [diagonals[0]]
    factored = factor(0, layout, tables, diagonals[0], [])

    sums = source_sums(soon, table, first, second, heads, factored[0], chips)
    whole, _ = scatter_sum(sums[0], sums[1], place, col_count)
    early = targets[:soon] - whole.reshape(targets[:soon].shape)
    starts = [early[s] for s in range(soon)]
    sent_rest = place
    if soon < sections:
        whole, sent_rest = scatter_sum(sums[2], sums[3], whole, col_count)
        late = targets[soon:] - whole.reshape(targets[soon:].shape)
        starts += [late[s - soon] for s in range(soon, sections)]

    later = [None] * sections
    pairs = [(s, j) for s in range(1, min(soon, last)) for j in range(1, sections - s)]
    middle = range(1, min(soon + 1, sections))
    if last:
        group = known_blocks(layout, middle, pairs, tables, place, targets, total, early)
        whole = sum_rows(lax.all_gather(group, "row", axis=0), place)
        if pairs:
            later[1] = whole[: len(pairs)]
        diagonals += [whole[len(pairs) + n] for n in range(len(middle))]

    results, children = [], []
    for s in range(sections):
        upper, inverse = factored
        if s > 0:
            upper, inverse = factor(s, layout, tables, diagonals[s], children)
        if s == soon and s < last:
            spread = sum_rows(gathered, upper)
            diagonals += [spread[len(padded) + n] for n in range(len(final))]
            for t in range(soon, last):
                at = pairs.index((t, 1))
                later[t] = spread[at : at + last - t]
        made = panel_blocks(
            s, layout, tables, sent_rest if s == 0 else place, starts[s],
            later[s], s < last, inverse, upper, children
        )
        results.append(made[0])
        if s < last:
            message = made[1]
            if s == 0:
                whole = lax.all_gather(message, "row", axis=0)
                message = first_message(layout, tables, whole, message)
                pairs = [(t, j) for t in range(soon, last) for j in range(1, sections - t)]
                final = range(len(diagonals), sections)
                if pairs:
                    padded = pairs + pairs[:1] * (4 - len(pairs) - len(final))
                    known = known_blocks(
                        layout, final, padded, tables, whole, targets, total, late, soon
                    )
                    gathered = lax.all_gather(known, "row", axis=0)
            children = gather_columns(message, col_count)
    return jnp.stack(results)[:, None]


def solution(mesh):
    return jax.shard_map(
        local,
        mesh=mesh,
        in_specs=(
            P(None, "col", "row", None),
            P("col", "row", None),
            P("col"),
            P("col", None),
            P("col", None, "row"),
            P(),
            P(),
            P(None, None, "row"),
        ),
        out_specs=P(None, "col", "row", None),
        check_vma=False,
    )
```

```python
import functools

import jax
import jax.numpy as jnp
from jax import lax
from jax.experimental import pallas as pl
from jax.experimental.pallas import tpu as pltpu
from jax.sharding import PartitionSpec as P

F32 = jnp.float32
BF16 = jnp.bfloat16
HIGHEST = lax.Precision.HIGHEST
CHUNK = 8
PANEL = 32
MIB = 1024 * 1024


def vmem():
    return pl.BlockSpec(memory_space=pltpu.VMEM)


def smem():
    return pl.BlockSpec(memory_space=pltpu.SMEM)


def params(mib):
    return pltpu.CompilerParams(vmem_limit_bytes=mib * MIB)


def cost(flops, size):
    return pl.CostEstimate(flops=flops, bytes_accessed=size, transcendentals=0)


def times_transposed(a, b, precision=None):
    return lax.dot_general(
        a, b, (((1,), (1,)), ((), ())), precision=precision, preferred_element_type=F32
    )


def transposed_times(a, b):
    return lax.dot_general(a, b, (((0,), (0,)), ((), ())), preferred_element_type=F32)


def slot_column(slot, chips, own):
    return own ^ (2 * (slot % chips) + slot // chips)


def swap(x, axis, size, mask):
    return lax.ppermute(x, axis, [(i, i ^ mask) for i in range(size)])


def gather_columns(x, col_count):
    chips = col_count // 2
    same = [x] + [swap(x, "col", col_count, 2 * m) for m in range(1, chips)]
    return same + [swap(y, "col", col_count, 1) for y in same]


def halves_kernel(own, other, after, *outs):
    del after
    for m, out in enumerate(outs):
        out[...] = own[m] + other[m]


def scatter_sum(other_half, own_half, after, col_count):
    chips, *shape = own_half.shape
    swapped = swap(other_half, "col", col_count, 1)
    halves = pl.pallas_call(
        halves_kernel,
        in_specs=[vmem(), vmem(), pl.BlockSpec(memory_space=pl.ANY)],
        out_specs=[vmem()] * chips,
        out_shape=[jax.ShapeDtypeStruct(shape, F32)] * chips,
        compiler_params=params(12 * own_half.size // MIB + 4),
        cost_estimate=cost(own_half.size, 12 * own_half.size),
        name="halves",
    )(own_half, swapped, after)
    whole = halves[0]
    for m in range(1, chips):
        whole = whole + swap(halves[m], "col", col_count, 2 * m)
    return whole, halves[0]


class Tables:
    def __init__(self, sections, col_count, blocks):
        self.sections, self.col_count, self.blocks = sections, col_count, blocks
        grid, kids = sections * sections, sections * col_count
        self.starts = {"mine": 0, "roots": grid}
        self.starts["picks"] = self.starts["roots"] + grid
        self.starts["ahead"] = self.starts["picks"] + grid
        self.starts["keep"] = self.starts["ahead"] + kids * sections
        self.starts["into"] = self.starts["keep"] + kids * blocks
        self.size = self.starts["into"] + kids * blocks

    def at(self, name, s, *rest):
        place = s
        widths = {"ahead": (self.col_count, self.sections)}.get(name, (self.col_count, self.blocks))
        if name in ("mine", "roots", "picks"):
            widths = (self.sections,)
        for index, width in zip(rest, widths):
            place = place * width + index
        return self.starts[name] + place


def tables_kernel(layout, place, diag, parent, chain, out):
    sections, col_count, local_blocks = layout.sections, layout.col_count, layout.blocks
    chips = col_count // 2
    own = place[0]
    row = place[1]

    def path(s, column):
        columns = [column]
        for t in range(s, sections - 1):
            columns.append(parent[t, columns[-1]])
        return columns

    def block_of(s, columns, j):
        if j == 0:
            return jnp.int32(0)
        if j == 1:
            return jnp.int32(1)
        wanted = block_of(s + 1, columns[1:], j - 1)
        group = diag[s + j, columns[j]]
        found = jnp.int32(0)
        for q in range(1, local_blocks):
            found = jnp.where(chain[group, s, columns[0], q] == wanted, q, found)
        return found

    for s in range(sections):
        columns = path(s, own)
        for j in range(sections - s):
            group = diag[s + j, columns[j]]
            out[layout.at("mine", s, j)] = jnp.where(group == row, 1, 0)
            out[layout.at("roots", s, j)] = group
            out[layout.at("picks", s, j)] = block_of(s, columns, j)
    for s in range(1, sections):
        for slot in range(col_count):
            child = slot_column(slot, chips, own)
            hit = parent[s - 1, child] == own
            columns = path(s - 1, child)
            for j in range(sections - s):
                block = block_of(s - 1, columns, j + 1)
                group = diag[s + j, columns[j + 1]]
                left_out = (block == 0) & (group == diag[s - 1, child])
                out[layout.at("ahead", s, slot, j)] = jnp.where(
                    hit & jnp.logical_not(left_out), 1, 0
                )
            for q in range(local_blocks):
                left_out = (diag[s - 1, child] == row) & (q == 0)
                out[layout.at("keep", s, slot, q)] = jnp.where(
                    hit & jnp.logical_not(left_out), 1, 0
                )
                out[layout.at("into", s, slot, q)] = chain[row, s - 1, child, q]


def split_kernel(index, source, *outs):
    share = outs[0].shape[0]
    for k, out in enumerate(outs):
        for m in range(share):
            out[m] = source[index[k * share + m]]


def split_panels(source, index, block, width, parts):
    share = index.shape[0] // parts
    shape = (share, width, source.shape[2])
    return pl.pallas_call(
        split_kernel,
        grid_spec=pltpu.PrefetchScalarGridSpec(
            num_scalar_prefetch=1,
            grid=(1,),
            in_specs=[
                pl.BlockSpec((source.shape[0], width, source.shape[2]), lambda g, a: (0, block, 0))
            ],
            out_specs=[pl.BlockSpec(shape, lambda g, a: (0, 0, 0))] * parts,
        ),
        out_shape=[jax.ShapeDtypeStruct(shape, source.dtype)] * parts,
        compiler_params=params(48),
        cost_estimate=cost(0, 4 * index.shape[0] * width * source.shape[2]),
        name="split_panels",
    )(index, source)


def merge_kernel(index, *refs):
    parts, (out, work) = refs[:-2], refs[-2:]
    share = parts[0].shape[0]
    for k, part in enumerate(parts):
        work[k * share : (k + 1) * share] = part[...]
    for i in range(out.shape[0]):
        out[i] = work[index[i]]


def merge_panels(parts, index):
    share, width, _ = parts[0].shape
    count = index.shape[0]
    return pl.pallas_call(
        merge_kernel,
        in_specs=[smem()] + [vmem()] * len(parts),
        out_specs=vmem(),
        out_shape=jax.ShapeDtypeStruct((count,) + parts[0].shape[1:], parts[0].dtype),
        scratch_shapes=[pltpu.VMEM((len(parts) * share,) + parts[0].shape[1:], parts[0].dtype)],
        compiler_params=params(16),
        cost_estimate=cost(0, 8 * count * width * width),
        name="merge_panels",
    )(index, *parts)


def sum_kernel(after, x, out):
    del after
    total = x[0]
    for r in range(1, x.shape[0]):
        total = total + x[r]
    out[...] = total


def sum_rows(x, after):
    return pl.pallas_call(
        sum_kernel,
        in_specs=[pl.BlockSpec(memory_space=pl.ANY), vmem()],
        out_specs=vmem(),
        out_shape=jax.ShapeDtypeStruct(x.shape[1:], x.dtype),
        compiler_params=params(8),
        cost_estimate=cost(x.size, 4 * x.size),
        name="sum_rows",
    )(after, x)


def diagonal_kernel(table, heads, other, own, total):
    g = pl.program_id(0)
    chips = own.shape[0]
    sections = table.shape[0]

    @pl.when(g == 0)
    def _():
        total[...] = jnp.zeros_like(total)

    for t in range(heads.shape[0]):
        product = times_transposed(heads[t], heads[t])
        for s in range(sections):
            total[table[s, 0, g * heads.shape[0] + t], s] += product

    @pl.when(g == pl.num_programs(0) - 1)
    def _():
        own[...] = total[:chips]
        other[...] = total[chips : 2 * chips]


def diagonal_sums(table, heads, chips):
    count, width, _ = heads.shape
    sections = table.shape[0]
    chunk = min(CHUNK, count)
    half = (chips, sections, width, width)
    out = jax.ShapeDtypeStruct(half, F32)
    return pl.pallas_call(
        diagonal_kernel,
        grid_spec=pltpu.PrefetchScalarGridSpec(
            num_scalar_prefetch=1,
            grid=(count // chunk,),
            in_specs=[pl.BlockSpec((chunk, width, width), lambda g, a: (g, 0, 0))],
            out_specs=[pl.BlockSpec(half, lambda g, a: (0, 0, 0, 0))] * 2,
            scratch_shapes=[pltpu.VMEM((2 * chips + 1,) + half[1:], F32)],
        ),
        out_shape=[out, out],
        compiler_params=params(6 * chips * sections * width * width * 4 // MIB + 8),
        cost_estimate=cost(count * width * width * width * 4, count * width * width * 4),
        name="diagonal_sums",
    )(table, heads)


def source_kernel(soon, table, first, second, heads, after, other, own, *refs):
    del after
    rest, total = refs[:-1], refs[-1]
    g = pl.program_id(0)
    chunk, width, _ = first.shape
    chips = own.shape[0]
    blocks = second.shape[1] + 1
    sections = table.shape[0]

    @pl.when(g == 0)
    def _():
        total[...] = jnp.zeros_like(total)

    for t in range(chunk):
        i = g * chunk + t
        panel = jnp.concatenate([first[t]] + [second[t, q] for q in range(blocks - 1)], axis=0)
        for begin in range(0, sections, 2):
            steps = range(begin, min(begin + 2, sections))
            stacked = jnp.concatenate([heads[table[s, 1, i], t] for s in steps], axis=0)
            product = times_transposed(panel, stacked)
            for k, s in enumerate(steps):
                slot = table[s, 0, i]
                for q in range(blocks):
                    total[slot, s * blocks + table[s, 2 + q, i]] += product[
                        q * width : (q + 1) * width, k * width : (k + 1) * width
                    ]

    @pl.when(g == pl.num_programs(0) - 1)
    def _():
        other[...] = total[chips : 2 * chips, : soon * blocks]
        own[...] = total[:chips, : soon * blocks]
        if rest:
            rest[0][...] = total[chips : 2 * chips, soon * blocks :]
            rest[1][...] = total[:chips, soon * blocks :]


def source_sums(soon, table, first, second, heads, after, chips):
    count, width, _ = first.shape
    blocks = 1 + second.shape[1]
    sections = table.shape[0]
    chunk = min(CHUNK, count)
    shapes = [(chips, soon * blocks, width, width)] * 2
    if soon < sections:
        shapes += [(chips, (sections - soon) * blocks, width, width)] * 2
    size = 4 * chips * sections * blocks * width * width
    return pl.pallas_call(
        functools.partial(source_kernel, soon),
        grid_spec=pltpu.PrefetchScalarGridSpec(
            num_scalar_prefetch=1,
            grid=(count // chunk,),
            in_specs=[
                pl.BlockSpec((chunk, width, width), lambda g, a: (g, 0, 0)),
                pl.BlockSpec((chunk, blocks - 1, width, width), lambda g, a: (g, 0, 0, 0)),
                pl.BlockSpec((heads.shape[0], chunk, width, width), lambda g, a: (0, g, 0, 0)),
                pl.BlockSpec(memory_space=pl.ANY),
            ],
            out_specs=[pl.BlockSpec(shape, lambda g, a: (0, 0, 0, 0)) for shape in shapes],
            scratch_shapes=[pltpu.VMEM((2 * chips, sections * blocks, width, width), F32)],
        ),
        out_shape=[jax.ShapeDtypeStruct(shape, F32) for shape in shapes],
        compiler_params=params(6 * size // MIB + 38),
        cost_estimate=cost(
            count * blocks * width * width * width * 2 * sections, count * width * width * 12
        ),
        name="source_sums",
    )(table, first, second, heads, after)


def known_kernel(layout, begin, steps, pairs, tables, after, targets, sums, *refs):
    del after
    starts, out = refs[:-1], refs[-1]
    zeros = jnp.zeros(out.shape[1:], F32)
    n = 0
    for s, j in pairs:
        block = starts[0][s - begin, tables[layout.at("picks", s, j)]]
        out[n] = jnp.where(tables[layout.at("mine", s, j)] > 0, block, zeros)
        n += 1
    for s in steps:
        block = targets[s, 0] - sums[s]
        out[n] = jnp.where(tables[layout.at("mine", s, 0)] > 0, block, zeros)
        n += 1


def known_blocks(
    layout, steps, pairs, tables, after, targets, sums, starts=None, begin=0
):
    width = targets.shape[-1]
    arrays = [targets, sums] + ([] if starts is None else [starts])
    shape = (len(steps) + len(pairs), width, width)
    return pl.pallas_call(
        functools.partial(known_kernel, layout, begin, steps, pairs),
        in_specs=[smem(), pl.BlockSpec(memory_space=pl.ANY)] + [vmem()] * len(arrays),
        out_specs=vmem(),
        out_shape=jax.ShapeDtypeStruct(shape, F32),
        compiler_params=params(8),
        cost_estimate=cost(targets.size, 4 * targets.size),
        name="known_blocks",
    )(tables, after, *arrays)


def message_kernel(layout, tables, whole, own, out):
    ahead = layout.sections - 1
    for j in range(ahead):
        group = tables[layout.at("roots", 0, j + 1)]
        out[j] = whole[group, tables[layout.at("picks", 0, j + 1)]]
    out[ahead:] = own[...]


def first_message(layout, tables, whole, own):
    blocks, width, _ = own.shape
    shape = (layout.sections - 1 + blocks, width, width)
    return pl.pallas_call(
        functools.partial(message_kernel, layout),
        in_specs=[smem(), vmem(), vmem()],
        out_specs=vmem(),
        out_shape=jax.ShapeDtypeStruct(shape, own.dtype),
        compiler_params=params(4),
        cost_estimate=cost(own.size, 8 * own.size),
        name="first_message",
    )(tables, whole, own)


def split(x):
    high = x.astype(BF16)
    rest = x - high.astype(F32)
    middle = rest.astype(BF16)
    low = (rest - middle.astype(F32)).astype(BF16)
    return high, middle, low


def factor_kernel(step, layout, tables, start, *refs):
    children, (upper, inverse, work) = refs[:-3], refs[-3:]
    width = start.shape[0]
    work[:, :width] = start[...]
    for slot, child in enumerate(children):

        @pl.when(tables[layout.at("ahead", step, slot, 0)] > 0)
        def _(child=child):
            work[:, :width] -= times_transposed(child[0], child[0])

    rows = lax.broadcasted_iota(jnp.int32, (width, width), 0)
    columns = lax.broadcasted_iota(jnp.int32, (width, width), 1)
    work[:, width:] = (rows == columns).astype(F32)
    groups = range(PANEL // 8)
    sub = lax.broadcasted_iota(jnp.int32, (8, 1), 0)
    for first in range(0, width, PANEL):
        last = first + PANEL
        slab = [work[first + 8 * g : first + 8 * g + 8, :] for g in groups]
        spans = [
            {
                g: jnp.broadcast_to(slab[g][:, first + k : first + k + 1], (8, width))
                for g in groups
                if g >= k // 8
            }
            for k in range(PANEL)
        ]
        scale = [jnp.zeros((8, 1), F32) for _ in groups]
        for j in range(PANEL):
            here, row = divmod(j, 8)
            pivot = spans[j][here][row : row + 1, :]
            inverted = 1.0 / pivot
            ratio = {g: span * inverted for g, span in spans[j].items()}
            ratio[here] = jnp.where(sub > row, ratio[here], 0.0)
            for k in range(j + 1, PANEL):
                crossing = spans[j][k // 8][k % 8 : k % 8 + 1, :]
                for g in spans[k]:
                    spans[k][g] = spans[k][g] - ratio[g] * crossing
            line = slab[here][row : row + 1, :]
            for g in ratio:
                slab[g] = slab[g] - jnp.concatenate([ratio[g], ratio[g]], axis=1) * line
            scale[here] = jnp.where(sub == row, lax.rsqrt(pivot[:, 0:1]), scale[here])
        slab = jnp.concatenate([slab[g] * scale[g] for g in groups], axis=0)
        work[first:last, :] = slab
        if last < width:
            high, middle, low = split(slab)
            left = jnp.concatenate([high, high, middle, middle, high, low], axis=0)
            right = jnp.concatenate([high, middle, high, middle, low, high], axis=0)
            work[last:, :] = work[last:, :] - transposed_times(left[:, last:width], right)
    upper[...] = jnp.where(rows <= columns, work[:, :width], 0.0)
    inverse[...] = work[:, width:]


def factor(step, layout, tables, start, children):
    width = start.shape[0]
    out = jax.ShapeDtypeStruct((width, width), F32)
    return pl.pallas_call(
        functools.partial(factor_kernel, step, layout),
        in_specs=[smem(), vmem()] + [vmem()] * len(children),
        out_specs=[vmem(), vmem()],
        out_shape=[out, out],
        scratch_shapes=[pltpu.VMEM((width, 2 * width), F32)],
        compiler_params=params(8),
        cost_estimate=cost(width * width * width * 200, 16 * width * width),
        name="factor",
    )(tables, start, *children)


def blocks_kernel(step, layout, ahead, send, tables, after, start, inverse, upper, *refs):
    del after
    work, refs = refs[-1], refs[:-1]
    rounded, refs = (refs[-1], refs[:-1]) if send else (None, refs)
    out, refs = refs[-1], refs[:-1]
    later, children = (refs[0], refs[1:]) if ahead else (None, refs)
    blocks, width = start.shape[0], start.shape[1]
    for j in range(ahead):
        work[j] = later[j]
    work[ahead:] = start[...]
    for slot, child in enumerate(children):
        skipped = child.shape[0] - blocks
        for j in range(ahead):

            @pl.when(tables[layout.at("ahead", step, slot, j + 1)] > 0)
            def _(slot=slot, child=child, j=j):
                work[j] -= times_transposed(child[j + 1], child[0])

        for q in range(blocks):

            @pl.when(tables[layout.at("keep", step, slot, q)] > 0)
            def _(slot=slot, child=child, q=q):
                into = tables[layout.at("into", step, slot, q)]
                work[ahead + into] -= times_transposed(child[skipped + q], child[0])

    solved = times_transposed(
        work[...].reshape((ahead + blocks) * width, width), inverse[...], HIGHEST
    )
    out[...] = solved[ahead * width :]
    if send:
        rounded[...] = solved.astype(BF16).reshape(ahead + blocks, width, width)

    @pl.when(tables[layout.at("mine", step, 0)] > 0)
    def _():
        out[:width, :] = upper[...].T


def panel_blocks(step, layout, tables, after, start, later, send, inverse, upper, children):
    blocks, width, _ = start.shape
    ahead = 0 if later is None else later.shape[0]
    arrays = [start, inverse, upper] + ([later] if ahead else []) + list(children)
    out = [jax.ShapeDtypeStruct((blocks * width, width), F32)]
    if send:
        out.append(jax.ShapeDtypeStruct((ahead + blocks, width, width), BF16))
    return pl.pallas_call(
        functools.partial(blocks_kernel, step, layout, ahead, send),
        in_specs=[smem(), pl.BlockSpec(memory_space=pl.ANY)] + [vmem()] * len(arrays),
        out_specs=[vmem()] * len(out),
        out_shape=out,
        scratch_shapes=[pltpu.VMEM((blocks + ahead, width, width), F32)],
        compiler_params=params(12),
        cost_estimate=cost(start.size * 2000, start.size * 16),
        name="panel_blocks",
    )(tables, after, *arrays)


def local(targets, src_panels, live_counts, dest_owner, relative_map, diag_row, parent, chain_map):
    col_count = lax.axis_size("col")
    row_count = lax.axis_size("row")
    own = lax.axis_index("col")
    row_index = lax.axis_index("row")
    chips = col_count // 2
    src_count, _, width = src_panels.shape
    local_blocks = src_panels.shape[1] // width
    sections = targets.shape[0]
    targets = targets.reshape(sections, local_blocks, width, width)

    place = jnp.stack([own, row_index]).astype(jnp.int32)

    dealt = src_count // 2
    share = src_count // col_count
    facts = jnp.concatenate(
        [
            dest_owner.T,
            relative_map.transpose(1, 2, 0).reshape(sections * local_blocks, src_count),
            jnp.broadcast_to(live_counts, (1, src_count)),
        ],
        axis=0,
    ).astype(jnp.int32)
    facts = lax.all_gather(facts, "col", axis=0)
    counts = facts[:, -1, 0]
    columns_of = jnp.arange(col_count)
    offsets = jnp.sum(jnp.where(columns_of[None, :] < columns_of[:, None], counts[None, :], 0), axis=1)
    own_offset = jnp.sum(jnp.where(columns_of == own, offsets, 0))
    partner = jnp.bitwise_xor(columns_of, own)
    sent = (
        jnp.mod(partner - own_offset, col_count)[:, None] + col_count * jnp.arange(share)[None, :]
    ).reshape(-1)
    number = jnp.arange(dealt) * col_count + own
    source_column = jnp.sum(
        (offsets[None, :] <= number[:, None]).astype(jnp.int32), axis=1
    ) - 1
    index = number - jnp.sum(
        jnp.where(columns_of[None, :] == source_column[:, None], offsets[None, :], 0), axis=1
    )
    kept = jnp.bitwise_xor(source_column, own) * share + index // col_count

    def deal(block):
        parts = split_panels(src_panels, sent, block, width, col_count)
        parts = [swap(part, "col", col_count, k) if k else part for k, part in enumerate(parts)]
        return merge_panels(parts, kept)

    first = deal(0)
    heads = lax.all_gather(first, "row", axis=0)
    second = jnp.stack([deal(q) for q in range(1, local_blocks)], axis=1)

    chain = lax.all_gather(chain_map[None], "row", axis=0, tiled=True)
    layout = Tables(sections, col_count, local_blocks)
    tables = pl.pallas_call(
        functools.partial(tables_kernel, layout),
        in_specs=[smem()] * 4,
        out_specs=smem(),
        out_shape=jax.ShapeDtypeStruct((layout.size,), jnp.int32),
        name="tables",
    )(place, diag_row, parent, chain)

    facts = facts.transpose(0, 2, 1).reshape(col_count * src_count, -1)
    facts = facts[source_column * src_count + index]
    dest = facts[:, :sections].T
    target_blocks = facts[:, sections:-1].T.reshape(sections, local_blocks, dealt)
    offset = jnp.bitwise_xor(dest, own)
    slots = (offset % 2) * chips + offset // 2
    source_root = jnp.sum(
        jnp.where(dest[:, :, None] == columns_of, diag_row[:, None, :], 0), axis=-1
    )
    table = jnp.concatenate([slots[:, None], source_root[:, None], target_blocks], axis=1)
    held = jnp.where(source_root == row_index, slots, 2 * chips)[:, None]

    other, mine = diagonal_sums(held, first, chips)
    total, _ = scatter_sum(other, mine, place, col_count)

    def share(x):
        return jnp.sum(lax.all_gather(x, "row", axis=0), axis=0)

    last = sections - 1
    soon = min(2, sections)
    diagonals = share(known_blocks(layout, [0], [], tables, place, targets, total))
    diagonals = [diagonals[0]]
    factored = factor(0, layout, tables, diagonals[0], [])

    sums = source_sums(soon, table, first, second, heads, factored[0], chips)
    whole, _ = scatter_sum(sums[0], sums[1], place, col_count)
    early = targets[:soon] - whole.reshape(targets[:soon].shape)
    starts = [early[s] for s in range(soon)]
    sent_rest = place
    if soon < sections:
        whole, sent_rest = scatter_sum(sums[2], sums[3], whole, col_count)
        late = targets[soon:] - whole.reshape(targets[soon:].shape)
        starts += [late[s - soon] for s in range(soon, sections)]

    later = [None] * sections
    pairs = [(s, j) for s in range(1, min(soon, last)) for j in range(1, sections - s)]
    middle = range(1, min(soon + 1, sections))
    if last:
        group = known_blocks(layout, middle, pairs, tables, place, targets, total, early)
        whole = sum_rows(lax.all_gather(group, "row", axis=0), place)
        if pairs:
            later[1] = whole[: len(pairs)]
        diagonals += [whole[len(pairs) + n] for n in range(len(middle))]

    results, children = [], []
    for s in range(sections):
        upper, inverse = factored
        if s > 0:
            upper, inverse = factor(s, layout, tables, diagonals[s], children)
        if s == soon and s < last:
            spread = sum_rows(gathered, upper)
            diagonals += [spread[len(padded) + n] for n in range(len(final))]
            for t in range(soon, last):
                at = pairs.index((t, 1))
                later[t] = spread[at : at + last - t]
        made = panel_blocks(
            s, layout, tables, sent_rest if s == 0 else place, starts[s],
            later[s], s < last, inverse, upper, children
        )
        results.append(made[0])
        if s < last:
            message = made[1]
            if s == 0:
                whole = lax.all_gather(message, "row", axis=0)
                message = first_message(layout, tables, whole, message)
                pairs = [(t, j) for t in range(soon, last) for j in range(1, sections - t)]
                final = range(len(diagonals), sections)
                if pairs:
                    padded = pairs + pairs[:1] * (4 - len(pairs) - len(final))
                    known = known_blocks(
                        layout, final, padded, tables, whole, targets, total, late, soon
                    )
                    gathered = lax.all_gather(known, "row", axis=0)
            children = gather_columns(message, col_count)
    return jnp.stack(results)[:, None]


def solution(mesh):
    return jax.shard_map(
        local,
        mesh=mesh,
        in_specs=(
            P(None, "col", "row", None),
            P("col", "row", None),
            P("col"),
            P("col", None),
            P("col", None, "row"),
            P(),
            P(),
            P(None, None, "row"),
        ),
        out_specs=P(None, "col", "row", None),
        check_vma=False,
    )
```
